128 devices in a mesh: gx: 16 (over x_lo, y, core), gy: 8 (over z, x_hi).
Axes of the slice: x: 4 (x_hi: 2, x_lo: 2; x = x_hi * 2 + x_lo), y: 4, z: 4, core: 2. Of those that a mesh axis runs over, the one named last changes fastest.
Arguments:
- segment_wattage_table: float32 [524288, 128], P(('gx', 'gy')), may hold values from 0.05 to 2
- segment_target_tile: int32 [524288], P(('gx', 'gy')), may hold values from 0 to 127, as said below
- occupied_slot_tally: int32 [128], P(('gx', 'gy')), may hold values from 2048 to 4096, as said below
- segment_tile_position: int32 [524288], P(('gx', 'gy')), may hold values from 0 to 4095
- stratum_substance: int32 [8], replicated, may hold values from 0 to 3, as said below
- substance_transport_base: float32 [4], replicated, may hold values from 0.5 to 4
- substance_thermal_slope: float32 [4], replicated, may hold values from 0.2 to 1
- thermal_scaling_factor: float32 [8, 4096, 2048], P(None, 'gx', 'gy'), may hold values from 0.5 to 2
- starting_warmth_excess: float32 [8, 4096, 2048], P(None, 'gx', 'gy'), may hold values from 0.5 to 1.5
Outputs:
- site_wattage_field: float32 [8, 4096, 2048], P(None, 'gx', 'gy')
- final_warmth_field: float32 [8, 4096, 2048], P(None, 'gx', 'gy')
The draws below stay inside these ranges and needn't reach their ends.
Inputs may be any that keep to these rules, and one draw needn't show every extreme that they name: `segment_target_tile`: among the rows of one owner at most 48 name the same tile; one tile is named by exactly 48 live rows of every owner. `occupied_slot_tally`: some owner has all 4096 slots live. `stratum_substance`: every material is used by some layer.
All inputs are finite; a program needn't handle non-finite values.
Results may differ from the reference program's by a relative error of at most 0.0003.
Values sent between devices are 32-bit elements; how exact they have to be, the bound alone decides.
No kernel may reach another device: no remote copies, remote signals or barrier semaphores. Data moves between devices by JAX's collectives and lax.ppermute only.
A program may use at most 128 MiB of HBM per device.

```python
import math
import jax
import jax.numpy as jnp

CX = 256
CY = 256
STRATA_TOTAL = 8
RUN = 128
BLK_DEV = 4096
SWEEPS = 3
NMAT = 4
TILES = 128
CAP = 48
RUNS = 4096
LENGTH_FIRST = 4096
LENGTH_SECOND = 2048
N_GX = 16
N_GY = 8


def routing(key):
    key_count, key_hot, key_order, key_turn, key_full = jax.random.split(key, 5)
    counts = jax.random.randint(key_count, (TILES,), BLK_DEV // 2, BLK_DEV + 1)
    fullest = jax.random.randint(key_full, (), 0, TILES)
    counts = jnp.where(jnp.arange(TILES) == fullest, BLK_DEV, counts)
    hottest = jax.random.randint(key_hot, (), 0, TILES)
    turns = jax.random.randint(key_turn, (TILES, 1), 0, TILES - 1)
    slots = jnp.arange(BLK_DEV)[None, :]
    others = (hottest + 1 + (slots - CAP + turns) % (TILES - 1)) % TILES
    base = jnp.where(slots < CAP, hottest, others)
    scores = jax.random.randint(key_order, (TILES, BLK_DEV), 0, BLK_DEV) * BLK_DEV + slots
    scores = jnp.where(slots < counts[:, None], scores, BLK_DEV * BLK_DEV + slots)
    order = jnp.argsort(scores, axis=1, stable=True)
    dests = jnp.take_along_axis(base, order, axis=1)
    return (counts.astype(jnp.int32), dests.reshape(-1).astype(jnp.int32))


def draw_segment_target_tile(key, part):
    counts, dests = routing(key)
    return dests


def draw_occupied_slot_tally(key, part):
    counts, dests = routing(key)
    return counts


def draw_stratum_substance(key, part):
    key = jax.random.fold_in(key, 7)
    key_fill, key_perm = jax.random.split(key)
    extra = jax.random.randint(key_fill, (STRATA_TOTAL - NMAT,), 0, NMAT)
    listed = jnp.concatenate([jnp.arange(NMAT), extra])
    return jax.random.permutation(key_perm, listed).astype(jnp.int32)


def place_ends(result, stream_key, smallest, top_value):
    spot = [jax.random.randint(jax.random.fold_in(stream_key, axis), (), 0, length) for axis, length in enumerate(result.shape)]
    longest = result.shape.index(max(result.shape))
    beside = spot[:longest] + [(spot[longest] + 1) % result.shape[longest]] + spot[longest + 1:]
    return result.at[tuple(spot)].set(smallest).at[tuple(beside)].set(top_value)


def block_levels(own_key, extent, shards, low, top_value):
    gain = 1.0
    for position, shards_of in shards:
        draws = jax.random.uniform(jax.random.fold_in(jax.random.fold_in(own_key, 6), position), (shards_of,), jnp.float32, low / len(shards), top_value / len(shards))
        gain = gain * jnp.repeat(jnp.exp(draws), extent[position] // shards_of).reshape((-1,) + (1,) * (len(extent) - 1 - position))
    return gain


def setup_inputs(seed: int = 0) -> dict:
    key_of = jax.random.split(jax.random.key(seed), 10)
    return {
        "segment_wattage_table": jnp.clip(jnp.exp(math.log(2.0) - 3.6888794 * jax.random.uniform(key_of[0], (TILES * BLK_DEV, RUN), jnp.float32) ** block_levels(key_of[0], (TILES * BLK_DEV, RUN), ((0, 128),), -0.2, 0.2)), 0.05, 2.0),
        "segment_target_tile": draw_segment_target_tile(jax.random.fold_in(key_of[9], 71), 0),
        "occupied_slot_tally": draw_occupied_slot_tally(jax.random.fold_in(key_of[9], 71), 0),
        "segment_tile_position": place_ends(jax.random.randint(key_of[3], (TILES * BLK_DEV,), 0, RUNS), jax.random.fold_in(key_of[3], 1), 0, RUNS - 1).astype(jnp.int32),
        "stratum_substance": draw_stratum_substance(jax.random.fold_in(key_of[9], 71), 0),
        "substance_transport_base": jnp.clip(jnp.exp(jax.random.uniform(key_of[5], (NMAT,), jnp.float32, math.log(0.5), math.log(4.0))), 0.5, 4.0),
        "substance_thermal_slope": jnp.clip(jax.random.uniform(key_of[6], (NMAT,), jnp.float32, 0.2, 1.0), 0.2, 1.0),
        "thermal_scaling_factor": jnp.clip(jnp.exp(math.log(2.0) - 1.3862944 * jax.random.uniform(key_of[7], (STRATA_TOTAL, LENGTH_FIRST, LENGTH_SECOND), jnp.float32) ** block_levels(key_of[7], (STRATA_TOTAL, LENGTH_FIRST, LENGTH_SECOND), ((1, 16), (2, 8)), -0.2, 0.2)), 0.5, 2.0),
        "starting_warmth_excess": jnp.clip(0.5 + 1.0 * jax.random.uniform(key_of[8], (STRATA_TOTAL, LENGTH_FIRST, LENGTH_SECOND), jnp.float32) ** block_levels(key_of[8], (STRATA_TOTAL, LENGTH_FIRST, LENGTH_SECOND), ((1, 16), (2, 8)), -0.2, 0.2), 0.5, 1.5),
    }


vertical_ratio = 0.5
sink_value = 4.0


def harmonic(left, right):
    total = left + right
    return jnp.where(total > 0, 2.0 * left * right / jnp.where(total > 0, total, 1.0), 0.0)


def smoothing_sites(temp_pad, cond_pad, site_wattage_field, cooler_coupling_factor):
    center_t = temp_pad[:, 1:-1, 1:-1]
    center_k = cond_pad[:, 1:-1, 1:-1]
    numer = site_wattage_field
    denom = cooler_coupling_factor + jnp.zeros_like(center_t)
    lateral = ((temp_pad[:, :-2, 1:-1], cond_pad[:, :-2, 1:-1]), (temp_pad[:, 2:, 1:-1], cond_pad[:, 2:, 1:-1]),
               (temp_pad[:, 1:-1, :-2], cond_pad[:, 1:-1, :-2]), (temp_pad[:, 1:-1, 2:], cond_pad[:, 1:-1, 2:]))
    for other_t, other_k in lateral:
        face = harmonic(center_k, other_k)
        numer = numer + face * other_t
        denom = denom + face
    stack_t = jnp.pad(center_t, ((1, 1), (0, 0), (0, 0)))
    stack_k = jnp.pad(center_k, ((1, 1), (0, 0), (0, 0)))
    for other_t, other_k in ((stack_t[:-2], stack_k[:-2]), (stack_t[2:], stack_k[2:])):
        face = vertical_ratio * harmonic(center_k, other_k)
        numer = numer + face * other_t
        denom = denom + face
    return jnp.where(denom > 0, numer / jnp.where(denom > 0, denom, 1.0), 0.0)


def layer_tables(stratum_substance, substance_transport_base, substance_thermal_slope):
    matches = stratum_substance[:, None] == jnp.arange(NMAT, dtype=jnp.int32)[None, :]
    stratum_transport_factor = jnp.sum(jnp.where(matches, substance_transport_base[None, :], 0.0), axis=1).astype(jnp.float32)
    stratum_storage_factor = jnp.sum(jnp.where(matches, substance_thermal_slope[None, :], 0.0), axis=1).astype(jnp.float32)
    planes = jnp.arange(stratum_substance.shape[0], dtype=jnp.int32)
    cooler_coupling_factor = jnp.where(planes == 0, sink_value, 0.0).astype(jnp.float32)
    return stratum_transport_factor[:, None, None], stratum_storage_factor[:, None, None], cooler_coupling_factor[:, None, None]


def diffusion_step_rule(final_warmth_field, thermal_scaling_factor, stratum_transport_factor, stratum_storage_factor):
    return stratum_transport_factor * thermal_scaling_factor / (1.0 + stratum_storage_factor * final_warmth_field)


def reference(segment_wattage_table, segment_target_tile, occupied_slot_tally, segment_tile_position, stratum_substance, substance_transport_base, substance_thermal_slope, thermal_scaling_factor, starting_warmth_excess):
    slots = jnp.arange(BLK_DEV, dtype=jnp.int32)
    live = (slots[None, :] < occupied_slot_tally[:, None]).reshape(-1)
    target = jnp.where(live, segment_target_tile * RUNS + segment_tile_position, TILES * RUNS).astype(jnp.int32)
    rows = jnp.zeros((TILES * RUNS, RUN), jnp.float32).at[target].add(segment_wattage_table, mode="drop")
    site_wattage_field = rows.reshape(N_GX, N_GY, STRATA_TOTAL, CX, CY).transpose(2, 0, 3, 1, 4).reshape(STRATA_TOTAL, LENGTH_FIRST, LENGTH_SECOND)
    stratum_transport_factor, stratum_storage_factor, cooler_coupling_factor = layer_tables(stratum_substance, substance_transport_base, substance_thermal_slope)
    final_warmth_field = starting_warmth_excess
    segment_spans = ((0, 0), (1, 1), (1, 1))
    for counter in range(SWEEPS):
        neighbour_coupling_mean = diffusion_step_rule(final_warmth_field, thermal_scaling_factor, stratum_transport_factor, stratum_storage_factor)
        final_warmth_field = smoothing_sites(jnp.pad(final_warmth_field, segment_spans), jnp.pad(neighbour_coupling_mean, segment_spans), site_wattage_field, cooler_coupling_factor)
    return site_wattage_field, final_warmth_field
```

```python
import jax
import jax.numpy as jnp
from jax import lax
from jax.experimental import pallas as pl
from jax.experimental.pallas import tpu as pltpu
from jax.sharding import PartitionSpec as P

RUN = 128
SWEEPS = 3
CAP = 48
CHUNK = CAP + 1
LAYERS = 8
NX = 256
NY = 256
GROUPS = NX // 8
POSITIONS = LAYERS * NX * NY // RUN
ACCS = 4
WALL = 1e30
BASE = 16
ROWS = 280
VMEM_LIMIT = 60 * 1024 * 1024
F32 = jnp.float32
BF16 = jnp.bfloat16


def iota(shape, dim):
    return lax.broadcasted_iota(jnp.int32, shape, dim)


def pack_kernel(tally_ref, target_ref, place_ref, table_ref, out_ref, dest_v, dest_s, sem):
    tally = tally_ref[0]
    tiles = 128
    sub = iota((tiles, RUN), 0)
    lane = iota((1, RUN), 1)
    tri_row = iota((RUN, 2 * RUN), 0)
    tri_col = iota((RUN, 2 * RUN), 1)
    tri = jnp.where((tri_row <= tri_col) | (tri_col >= RUN), 1.0, 0.0).astype(BF16)

    def rank_group(g, carry):
        seen, placed = carry
        live = (lane + g * RUN) < tally
        tgt = target_ref[pl.ds(g, 1), :]
        match = sub == jnp.where(live, tgt, -1)
        onehot = jnp.where(match, 1.0, 0.0)
        run = jnp.dot(onehot.astype(BF16), tri, preferred_element_type=F32)
        rank = jnp.sum(jnp.where(match, seen + run[:, :RUN], 0.0), axis=0, keepdims=True)
        rank = rank.astype(jnp.int32) - 1
        dest_v[pl.ds(g, 1), :] = jnp.where(live, tgt * CHUNK + rank, CAP)
        spot = place_ref[pl.ds(g, 1), :]
        spot = (spot & ~15) | ((spot & 1) << 3) | ((spot >> 1) & 7)
        spot = spot + 1
        digits = jnp.where(sub < 64, spot & 63, spot >> 6)
        chosen = jnp.where((sub & 63) == rank, digits, 0).astype(F32)
        placed = placed + lax.dot_general(
            onehot.astype(BF16),
            chosen.astype(BF16),
            (((1,), (1,)), ((), ())),
            preferred_element_type=F32,
        )
        return seen + run[:, RUN:], placed

    zero = jnp.zeros((tiles, RUN), F32)
    seen, placed = lax.fori_loop(0, target_ref.shape[0], rank_group, (zero, zero))
    placed = placed + 64.0 * pltpu.roll(placed, 64, 1)
    copy = pltpu.make_async_copy(dest_v, dest_s, sem)
    copy.start()
    copy.wait()

    def move(j, _):
        for k in range(16):
            row = j * 16 + k
            d = dest_s[j // 8, (j % 8) * 16 + k]
            out_ref[pl.ds(d, 1), :] = table_ref[pl.ds(row, 1), :]
        return 0

    lax.fori_loop(0, (tally + 15) // 16, move, 0)
    for t in range(tiles):
        out_ref[t * CHUNK + CAP : t * CHUNK + CAP + 1, :] = placed[t : t + 1, :]


def pack(tally, target, place, table):
    tiles = 128
    return pl.pallas_call(
        pack_kernel,
        out_shape=jax.ShapeDtypeStruct((tiles * CHUNK, RUN), F32),
        in_specs=[
            pl.BlockSpec(memory_space=pltpu.SMEM),
            pl.BlockSpec(memory_space=pltpu.VMEM),
            pl.BlockSpec(memory_space=pltpu.VMEM),
            pl.BlockSpec(memory_space=pltpu.VMEM),
        ],
        out_specs=pl.BlockSpec(memory_space=pltpu.VMEM),
        scratch_shapes=[
            pltpu.VMEM((32, RUN), jnp.int32),
            pltpu.SMEM((32, RUN), jnp.int32),
            pltpu.SemaphoreType.DMA,
        ],
        compiler_params=pltpu.CompilerParams(vmem_limit_bytes=VMEM_LIMIT),
    )(tally, target, place, table)


def fold_left(kept, value, g, slot):
    return jnp.where(slot == g, pltpu.roll(value, (4 * g) % RUN, 1), kept)


def fold_right(kept, value, g, slot):
    return jnp.where(slot == g, pltpu.roll(value, (4 * g + 4) % RUN, 1), kept)


def prepare_kernel(
    kind_ref, base_ref, warmth_ref, scale_ref, q_ref, left_ref, right_ref, low_ref, high_ref
):
    slot = iota((8, RUN), 1) // 4

    def layer(l, _):
        inverse = 1.0 / jnp.full((8, RUN), base_ref[kind_ref[l]], F32)
        sides = [jnp.zeros((8, RUN), F32) for _ in range(4)]
        for g in range(GROUPS):
            for h in range(2):
                cols = slice(h * RUN, (h + 1) * RUN)
                t = warmth_ref[l, 8 * g : 8 * g + 8, cols]
                q = inverse / scale_ref[l, 8 * g : 8 * g + 8, cols]
                q_ref[l, 8 * g : 8 * g + 8, cols] = q
                if h == 0:
                    sides[0] = fold_left(sides[0], t, g, slot)
                    sides[1] = fold_left(sides[1], q, g, slot)
                else:
                    sides[2] = fold_right(sides[2], t, g, slot)
                    sides[3] = fold_right(sides[3], q, g, slot)
                if g == 0:
                    low_ref[0, l, :, cols] = t[:4]
                    low_ref[1, l, :, cols] = q[:4]
                if g == GROUPS - 1:
                    high_ref[0, l, :, cols] = t[4:]
                    high_ref[1, l, :, cols] = q[4:]
        left_ref[0, l] = sides[0]
        left_ref[1, l] = sides[1]
        right_ref[0, l] = sides[2]
        right_ref[1, l] = sides[3]
        return 0

    lax.fori_loop(0, LAYERS, layer, 0)


def prepare(kind, base, warmth, scale):
    vmem = pl.BlockSpec(memory_space=pltpu.VMEM)
    smem = pl.BlockSpec(memory_space=pltpu.SMEM)
    return pl.pallas_call(
        prepare_kernel,
        out_shape=(
            jax.ShapeDtypeStruct(warmth.shape, F32),
            jax.ShapeDtypeStruct((2, LAYERS, 8, RUN), F32),
            jax.ShapeDtypeStruct((2, LAYERS, 8, RUN), F32),
            jax.ShapeDtypeStruct((2, LAYERS, 4, NY), F32),
            jax.ShapeDtypeStruct((2, LAYERS, 4, NY), F32),
        ),
        in_specs=[smem, smem, vmem, vmem],
        out_specs=(vmem,) * 5,
        compiler_params=pltpu.CompilerParams(vmem_limit_bytes=VMEM_LIMIT),
        cost_estimate=pl.CostEstimate(flops=8000000, bytes_accessed=6300000, transcendentals=0),
    )(kind, base, warmth, scale)


def gather_kernel(
    inc_ref, left_in, right_in, low_in, high_in,
    field_ref, left_ref, right_ref, low_ref, high_ref,
    acc0, acc1, acc2, acc3, spot_v, spot_s, sem,
):
    accs = (acc0, acc1, acc2, acc3)
    tiles = 128
    for t in range(tiles):
        row = inc_ref[t * CHUNK + CAP : t * CHUNK + CAP + 1, :]
        spot_v[t : t + 1, :] = jnp.where(row > 0.5, row.astype(jnp.int32) - 1, POSITIONS)
    copy = pltpu.make_async_copy(spot_v, spot_s, sem)
    copy.start()

    def clear(i, _):
        for acc in accs:
            acc[pl.ds(pl.multiple_of(i * 64, 64), 64), :] = jnp.zeros((64, RUN), F32)
        return 0

    lax.fori_loop(0, POSITIONS // 64, clear, 0)
    copy.wait()

    def source(s, _):
        for p in range(CAP):
            o = spot_s[s, p]
            acc = accs[p % ACCS]
            acc[pl.ds(o, 1), :] += inc_ref[pl.ds(s * CHUNK + p, 1), :]
        return 0

    lax.fori_loop(0, tiles, source, 0)
    left_ref[0:2] = left_in[...]
    right_ref[0:2] = right_in[...]
    low_ref[0:2] = low_in[...]
    high_ref[0:2] = high_in[...]
    slot = iota((8, RUN), 1) // 4

    def layer(l, _):
        sides = [jnp.zeros((8, RUN), F32) for _ in range(2)]
        for g in range(GROUPS):
            for h in range(2):
                cols = slice(h * RUN, (h + 1) * RUN)
                start = pl.multiple_of(l * 512 + g * 16 + h * 8, 8)
                total = (acc0[pl.ds(start, 8), :] + acc1[pl.ds(start, 8), :]) + (
                    acc2[pl.ds(start, 8), :] + acc3[pl.ds(start, 8), :]
                )
                field_ref[l, 8 * g : 8 * g + 8, cols] = total
                if h == 0:
                    sides[0] = fold_left(sides[0], total, g, slot)
                else:
                    sides[1] = fold_right(sides[1], total, g, slot)
                if g == 0:
                    low_ref[2, l, :, cols] = total[:4]
                if g == GROUPS - 1:
                    high_ref[2, l, :, cols] = total[4:]
        left_ref[2, l] = sides[0]
        right_ref[2, l] = sides[1]
        return 0

    lax.fori_loop(0, LAYERS, layer, 0)


def gather(incoming, left, right, low, high):
    vmem = pl.BlockSpec(memory_space=pltpu.VMEM)
    return pl.pallas_call(
        gather_kernel,
        out_shape=(
            jax.ShapeDtypeStruct((LAYERS, NX, NY), F32),
            jax.ShapeDtypeStruct((3, LAYERS, 8, RUN), F32),
            jax.ShapeDtypeStruct((3, LAYERS, 8, RUN), F32),
            jax.ShapeDtypeStruct((3, LAYERS, 4, NY), F32),
            jax.ShapeDtypeStruct((3, LAYERS, 4, NY), F32),
        ),
        in_specs=[vmem] * 5,
        out_specs=(vmem,) * 5,
        scratch_shapes=[pltpu.VMEM((POSITIONS + 8, RUN), F32)] * ACCS
        + [
            pltpu.VMEM((128, RUN), jnp.int32),
            pltpu.SMEM((128, RUN), jnp.int32),
            pltpu.SemaphoreType.DMA,
        ],
        compiler_params=pltpu.CompilerParams(vmem_limit_bytes=VMEM_LIMIT),
    )(incoming, left, right, low, high)


def corner_kernel(from_left, from_right, low_in, high_in, low_ref, high_ref):
    slot = iota((8, RUN), 1) // 4
    for l in range(LAYERS):
        low = jnp.zeros((8, RUN), F32)
        high = jnp.zeros((8, RUN), F32)
        for q in range(3):
            for side, ref in enumerate((from_left, from_right)):
                k = 2 * q + side
                v = ref[q, l]
                low = jnp.where(slot == k, pltpu.roll(v, (4 * k) % RUN, 1), low)
                high = jnp.where(slot == k, pltpu.roll(v, (4 * k + 4) % RUN, 1), high)
            low_ref[l, :, q * NY : (q + 1) * NY] = low_in[q, l]
            high_ref[l, :, q * NY : (q + 1) * NY] = high_in[q, l]
        low_ref[l, :, 3 * NY :] = low[:4]
        high_ref[l, :, 3 * NY :] = high[4:]


def corners(from_left, from_right, low, high):
    vmem = pl.BlockSpec(memory_space=pltpu.VMEM)
    shape = jax.ShapeDtypeStruct((LAYERS, 4, 3 * NY + RUN), F32)
    return pl.pallas_call(
        corner_kernel,
        out_shape=(shape, shape),
        in_specs=[vmem] * 4,
        out_specs=(vmem,) * 2,
    )(from_left, from_right, low, high)


def sweep_kernel(
    kind_ref, slope_ref, flag_ref, warmth_hbm, q_hbm, field_hbm, from_left, from_right, from_low, from_high,
    out_hbm,
    warm_a, warm_b, q_ext, field_ext, r_row, f_row, g_row, sem,
):
    bodies = (warmth_hbm, q_hbm, field_hbm)
    exts = (warm_a, q_ext, field_ext)
    copies = []
    for k in range(3):
        for l in range(LAYERS):
            for h in range(2):
                copies.append(
                    pltpu.make_async_copy(
                        bodies[k].at[l, :, pl.ds(h * RUN, RUN)],
                        exts[k].at[l, h, pl.ds(BASE, NX), :],
                        sem.at[k, l, h],
                    )
                )
    for c in copies:
        c.start()
    has_left = flag_ref[0] > 0
    has_right = flag_ref[1] > 0
    has_low = flag_ref[2] > 0
    has_high = flag_ref[3] > 0
    fills = (0.0, WALL, 0.0)
    lane = iota((8, RUN), 1)
    first_half = lane < 64

    def halo(l, _):
        for k in range(3):
            v = jnp.where(has_left, from_left[k, l], fills[k])
            w = jnp.where(has_right, from_right[k, l], fills[k])
            v = pltpu.roll(v, RUN - 4, 1)
            for g in range(GROUPS):
                shift = (RUN - 4 * g) % RUN
                third = jnp.where(first_half, pltpu.roll(w, shift, 1), pltpu.roll(v, shift, 1))
                exts[k][l, 2, BASE + 8 * g : BASE + 8 * g + 8, :] = third
            for ref, present, row in (
                (from_low, has_low, BASE - 4),
                (from_high, has_high, BASE + NX),
            ):
                for h in range(2):
                    main = ref[l, :, k * NY + h * RUN : k * NY + (h + 1) * RUN]
                    exts[k][l, h, row : row + 4, :] = jnp.where(present, main, fills[k])
                c = ref[l, :, 3 * NY :]
                cl = pltpu.roll(c, (RUN - (8 * k + 4)) % RUN, 1)
                cr = pltpu.roll(c, (RUN - (8 * k + 4)) % RUN, 1)
                cl = jnp.where(present & has_left, cl, fills[k])
                cr = jnp.where(present & has_right, cr, fills[k])
                exts[k][l, 2, row : row + 4, :] = jnp.where(first_half[:4], cr, cl)
        return 0

    lax.fori_loop(0, LAYERS, halo, 0)
    for c in copies:
        c.wait()

    last = lane == RUN - 1
    first = lane == 0

    def up(v):
        s = [pltpu.roll(x, RUN - 1, 1) for x in v]
        return [jnp.where(last, s[(h + 1) % 3], s[h]) for h in range(3)]

    def down(v):
        s = [pltpu.roll(x, 1, 1) for x in v]
        return [jnp.where(first, s[(h + 2) % 3], s[h]) for h in range(3)]

    def rcp(x):
        return pl.reciprocal(x, approx=True)

    slopes = [slope_ref[kind_ref[l]] for l in range(LAYERS)]

    def one_sweep(src, dst, top, stride):
        def load(ref, l, j):
            return [ref[l, h, pl.ds(top + j, 8, stride=stride), :] for h in range(3)]

        def resist(q, t, c):
            return [a * (1.0 + c * b) for a, b in zip(q, t)]

        for l in range(LAYERS):
            t0 = load(src, l, -1)
            t1 = load(src, l, 0)
            r0 = resist(load(q_ext, l, -1), t0, slopes[l])
            r1 = resist(load(q_ext, l, 0), t1, slopes[l])
            for h in range(3):
                g = rcp(r0[h] + r1[h])
                r_row[l, h] = r1[h]
                g_row[l, h] = g
                f_row[l, h] = g * (t1[h] - t0[h])

        def step(j, _):
            fz = gz = None
            t = load(src, 0, j)
            r = [r_row[0, h] for h in range(3)]
            for l in range(LAYERS):
                tn = load(src, l, j + 1)
                rn = resist(load(q_ext, l, j + 1), tn, slopes[l])
                power = load(field_ext, l, j)
                if l < LAYERS - 1:
                    t_above = load(src, l + 1, j)
                    r_above = [r_row[l + 1, h] for h in range(3)]
                net = []
                den = []
                for h in range(3):
                    gx = rcp(r[h] + rn[h])
                    fx = gx * (tn[h] - t[h])
                    net.append(fx - f_row[l, h])
                    den.append(gx + g_row[l, h])
                    r_row[l, h] = rn[h]
                    f_row[l, h] = fx
                    g_row[l, h] = gx
                ru = up(r)
                tu = up(t)
                gy = [rcp(r[h] + ru[h]) for h in range(3)]
                fy = [gy[h] * (tu[h] - t[h]) for h in range(3)]
                gd = down(gy)
                fd = down(fy)
                for h in range(3):
                    net[h] = net[h] + (fy[h] - fd[h])
                    den[h] = den[h] + (gy[h] + gd[h])
                if l > 0:
                    for h in range(3):
                        net[h] = net[h] - fz[h]
                        den[h] = den[h] + gz[h]
                else:
                    for h in range(3):
                        net[h] = net[h] - 2.0 * t[h]
                        den[h] = den[h] + 2.0
                if l < LAYERS - 1:
                    gz = [0.5 * rcp(r[h] + r_above[h]) for h in range(3)]
                    fz = [gz[h] * (t_above[h] - t[h]) for h in range(3)]
                    for h in range(3):
                        net[h] = net[h] + fz[h]
                        den[h] = den[h] + gz[h]
                for h in range(3):
                    fresh = t[h] + (0.5 * power[h] + net[h]) * rcp(den[h])
                    dst[l, h, pl.ds(top + j, 8, stride=stride), :] = fresh
                if l < LAYERS - 1:
                    t = t_above
                    r = r_above
            return 0

        lax.fori_loop(0, stride, step, 0)

    one_sweep(warm_a, warm_b, BASE - 4, 33)
    one_sweep(warm_b, warm_a, BASE - 4, 33)
    one_sweep(warm_a, warm_b, BASE - 4, 33)
    copies = [
        pltpu.make_async_copy(
            warm_b.at[l, h, pl.ds(BASE, NX), :],
            out_hbm.at[l, :, pl.ds(h * RUN, RUN)],
            sem.at[0, l, h],
        )
        for l in range(LAYERS)
        for h in range(2)
    ]
    for c in copies:
        c.start()
    for c in copies:
        c.wait()


def sweeps(kind, slope, flags, warmth, q, field, from_left, from_right, from_low, from_high):
    vmem = pl.BlockSpec(memory_space=pltpu.VMEM)
    smem = pl.BlockSpec(memory_space=pltpu.SMEM)
    hbm = pl.BlockSpec(memory_space=pl.ANY)
    ext = pltpu.VMEM((LAYERS, 3, ROWS, RUN), F32)
    row = pltpu.VMEM((LAYERS, 3, 8, RUN), F32)
    return pl.pallas_call(
        sweep_kernel,
        out_shape=jax.ShapeDtypeStruct((LAYERS, NX, NY), F32),
        in_specs=[smem, smem, smem, hbm, hbm, hbm, vmem, vmem, vmem, vmem],
        out_specs=hbm,
        scratch_shapes=[ext, ext, ext, ext, row, row, row, pltpu.SemaphoreType.DMA((3, LAYERS, 2))],
        compiler_params=pltpu.CompilerParams(vmem_limit_bytes=VMEM_LIMIT),
    )(kind, slope, flags, warmth, q, field, from_left, from_right, from_low, from_high)


def ring(axis):
    n = lax.axis_size(axis)
    return [(i, (i + 1) % n) for i in range(n)], [((i + 1) % n, i) for i in range(n)]


def per_device(
    segment_wattage_table,
    segment_target_tile,
    occupied_slot_tally,
    segment_tile_position,
    stratum_substance,
    substance_transport_base,
    substance_thermal_slope,
    thermal_scaling_factor,
    starting_warmth_excess,
):
    tiles = 128
    outgoing = pack(
        occupied_slot_tally,
        segment_target_tile.reshape(-1, RUN),
        segment_tile_position.reshape(-1, RUN),
        segment_wattage_table,
    )
    incoming = lax.all_to_all(
        outgoing.reshape(tiles, 1, CHUNK * RUN), ("gx", "gy"), split_axis=0, concat_axis=0, tiled=True
    ).reshape(tiles * CHUNK, RUN)
    q, left, right, low, high = prepare(
        stratum_substance, substance_transport_base, starting_warmth_excess, thermal_scaling_factor
    )
    field, left, right, low, high = gather(incoming, left, right, low, high)
    ahead, behind = ring("gy")
    from_left = lax.ppermute(right, "gy", ahead)
    from_right = lax.ppermute(left, "gy", behind)
    low, high = corners(from_left, from_right, low, high)
    ahead, behind = ring("gx")
    from_low = lax.ppermute(high, "gx", ahead)
    from_high = lax.ppermute(low, "gx", behind)
    i = lax.axis_index("gx")
    k = lax.axis_index("gy")
    flags = jnp.stack(
        [k > 0, k < lax.axis_size("gy") - 1, i > 0, i < lax.axis_size("gx") - 1]
    ).astype(jnp.int32)
    final = sweeps(
        stratum_substance,
        substance_thermal_slope,
        flags,
        starting_warmth_excess,
        q,
        field,
        from_left,
        from_right,
        from_low,
        from_high,
    )
    return field, final


def solution(mesh):
    return jax.shard_map(
        per_device,
        mesh=mesh,
        in_specs=(
            P(("gx", "gy"), None),
            P(("gx", "gy")),
            P(("gx", "gy")),
            P(("gx", "gy")),
            P(),
            P(),
            P(),
            P(None, "gx", "gy"),
            P(None, "gx", "gy"),
        ),
        out_specs=(P(None, "gx", "gy"), P(None, "gx", "gy")),
        check_vma=False,
    )
```

```python
import jax
import jax.numpy as jnp
from jax import lax
from jax.experimental import pallas as pl
from jax.experimental.pallas import tpu as pltpu
from jax.sharding import PartitionSpec as P

RUN = 128
SWEEPS = 3
CAP = 48
CHUNK = CAP + 1
LAYERS = 8
NX = 256
NY = 256
GROUPS = NX // 8
POSITIONS = LAYERS * NX * NY // RUN
ACCS = 8
WALL = 1e30
BASE = 16
ROWS = 280
VMEM_LIMIT = 60 * 1024 * 1024
F32 = jnp.float32
BF16 = jnp.bfloat16


def iota(shape, dim):
    return lax.broadcasted_iota(jnp.int32, shape, dim)


def pack_kernel(
    tally_ref, target_ref, place_ref, table_hbm, out_ref, table_ref, dest_v, dest_s, sem, table_sem
):
    load = pltpu.make_async_copy(table_hbm, table_ref, table_sem)
    load.start()
    tally = tally_ref[0]
    tiles = 128
    sub = iota((tiles, RUN), 0)
    lane = iota((1, RUN), 1)
    tri_row = iota((RUN, 2 * RUN), 0)
    tri_col = iota((RUN, 2 * RUN), 1)
    tri = jnp.where((tri_row <= tri_col) | (tri_col >= RUN), 1.0, 0.0).astype(BF16)

    def rank_group(g, carry):
        seen, placed = carry
        live = (lane + g * RUN) < tally
        tgt = target_ref[pl.ds(g, 1), :]
        match = sub == jnp.where(live, tgt, -1)
        onehot = jnp.where(match, 1.0, 0.0)
        run = jnp.dot(onehot.astype(BF16), tri, preferred_element_type=F32)
        rank = jnp.sum(jnp.where(match, seen + run[:, :RUN], 0.0), axis=0, keepdims=True)
        rank = rank.astype(jnp.int32) - 1
        dest_v[pl.ds(g, 1), :] = jnp.where(live, tgt * CHUNK + rank, CAP)
        spot = place_ref[pl.ds(g, 1), :]
        spot = (spot & ~15) | ((spot & 1) << 3) | ((spot >> 1) & 7)
        spot = spot + 1
        digits = jnp.where(sub < 64, spot & 63, spot >> 6)
        chosen = jnp.where((sub & 63) == rank, digits, 0).astype(F32)
        placed = placed + lax.dot_general(
            onehot.astype(BF16),
            chosen.astype(BF16),
            (((1,), (1,)), ((), ())),
            preferred_element_type=F32,
        )
        return seen + run[:, RUN:], placed

    zero = jnp.zeros((tiles, RUN), F32)
    seen, placed = lax.fori_loop(0, 32, rank_group, (zero, zero), unroll=32)
    placed = placed + 64.0 * pltpu.roll(placed, 64, 1)
    copy = pltpu.make_async_copy(dest_v, dest_s, sem)
    copy.start()
    copy.wait()

    load.wait()

    def move(g, _):
        for k in range(RUN):
            out_ref[pl.ds(dest_s[g, k], 1), :] = table_ref[pl.ds(g * RUN + k, 1), :]
        return 0

    lax.fori_loop(0, (tally + RUN - 1) // RUN, move, 0)
    for t in range(tiles):
        out_ref[t * CHUNK + CAP : t * CHUNK + CAP + 1, :] = placed[t : t + 1, :]


def pack(tally, target, place, table):
    tiles = 128
    return pl.pallas_call(
        pack_kernel,
        out_shape=jax.ShapeDtypeStruct((tiles * CHUNK, RUN), F32),
        in_specs=[
            pl.BlockSpec(memory_space=pltpu.SMEM),
            pl.BlockSpec(memory_space=pltpu.VMEM),
            pl.BlockSpec(memory_space=pltpu.VMEM),
            pl.BlockSpec(memory_space=pl.ANY),
        ],
        out_specs=pl.BlockSpec(memory_space=pltpu.VMEM),
        scratch_shapes=[
            pltpu.VMEM((32 * RUN, RUN), F32),
            pltpu.VMEM((32, RUN), jnp.int32),
            pltpu.SMEM((32, RUN), jnp.int32),
            pltpu.SemaphoreType.DMA,
            pltpu.SemaphoreType.DMA,
        ],
        compiler_params=pltpu.CompilerParams(vmem_limit_bytes=VMEM_LIMIT),
    )(tally, target, place, table)


def fold_left(kept, value, g, slot):
    return jnp.where(slot == g, pltpu.roll(value, (4 * g) % RUN, 1), kept)


def fold_right(kept, value, g, slot):
    return jnp.where(slot == g, pltpu.roll(value, (4 * g + 4) % RUN, 1), kept)


def prepare_kernel(
    kind_ref, base_ref, warmth_ref, scale_ref, q_ref, left_ref, right_ref, low_ref, high_ref
):
    slot = iota((8, RUN), 1) // 4

    def layer(l, _):
        inverse = 1.0 / jnp.full((8, RUN), base_ref[kind_ref[l]], F32)
        sides = [jnp.zeros((8, RUN), F32) for _ in range(4)]
        for g in range(GROUPS):
            for h in range(2):
                cols = slice(h * RUN, (h + 1) * RUN)
                t = warmth_ref[l, 8 * g : 8 * g + 8, cols]
                q = inverse / scale_ref[l, 8 * g : 8 * g + 8, cols]
                q_ref[l, 8 * g : 8 * g + 8, cols] = q
                if h == 0:
                    sides[0] = fold_left(sides[0], t, g, slot)
                    sides[1] = fold_left(sides[1], q, g, slot)
                else:
                    sides[2] = fold_right(sides[2], t, g, slot)
                    sides[3] = fold_right(sides[3], q, g, slot)
                if g == 0:
                    low_ref[0, l, :, cols] = t[:4]
                    low_ref[1, l, :, cols] = q[:4]
                if g == GROUPS - 1:
                    high_ref[0, l, :, cols] = t[4:]
                    high_ref[1, l, :, cols] = q[4:]
        left_ref[0, l] = sides[0]
        left_ref[1, l] = sides[1]
        right_ref[0, l] = sides[2]
        right_ref[1, l] = sides[3]
        return 0

    lax.fori_loop(0, LAYERS, layer, 0)


def prepare(kind, base, warmth, scale):
    vmem = pl.BlockSpec(memory_space=pltpu.VMEM)
    smem = pl.BlockSpec(memory_space=pltpu.SMEM)
    return pl.pallas_call(
        prepare_kernel,
        out_shape=(
            jax.ShapeDtypeStruct(warmth.shape, F32),
            jax.ShapeDtypeStruct((2, LAYERS, 8, RUN), F32),
            jax.ShapeDtypeStruct((2, LAYERS, 8, RUN), F32),
            jax.ShapeDtypeStruct((2, LAYERS, 4, NY), F32),
            jax.ShapeDtypeStruct((2, LAYERS, 4, NY), F32),
        ),
        in_specs=[smem, smem, vmem, vmem],
        out_specs=(vmem,) * 5,
        compiler_params=pltpu.CompilerParams(vmem_limit_bytes=VMEM_LIMIT),
        cost_estimate=pl.CostEstimate(flops=8000000, bytes_accessed=6300000, transcendentals=0),
    )(kind, base, warmth, scale)


def gather_kernel(
    flag_ref, inc_hbm, left_in, right_in, low_in, high_in,
    field_hbm, first_ref, second_ref, low_ref, high_ref,
    inc_ref, field_ref, spot_v, spot_s, inc_sem, spot_sem, field_sem, *accs,
):
    tiles = 128
    parts = 8
    size = tiles * CHUNK // parts
    loads = [
        pltpu.make_async_copy(
            inc_hbm.at[pl.ds(i * size, size), :], inc_ref.at[pl.ds(i * size, size), :], inc_sem.at[i]
        )
        for i in range(parts)
    ]
    for c in loads:
        c.start()

    def clear(i, _):
        for acc in accs:
            acc[pl.ds(pl.multiple_of(i * 64, 64), 64), :] = jnp.zeros((64, RUN), F32)
        return 0

    lax.fori_loop(0, POSITIONS // 64, clear, 0)
    for c in loads:
        c.wait()
    for t in range(tiles):
        row = inc_ref[t * CHUNK + CAP : t * CHUNK + CAP + 1, :]
        spot_v[t : t + 1, :] = jnp.where(row > 0.5, row.astype(jnp.int32) - 1, POSITIONS)
    copy = pltpu.make_async_copy(spot_v, spot_s, spot_sem)
    copy.start()
    copy.wait()

    def source(s, _):
        for p in range(CAP):
            acc = accs[p % ACCS]
            acc[pl.ds(spot_s[s, p], 1), :] += inc_ref[pl.ds(s * CHUNK + p, 1), :]
        return 0

    lax.fori_loop(0, tiles, source, 0)
    even = flag_ref[4] > 0

    def send(k, l, left, right):
        first_ref[k, l] = jnp.where(even, right, left)
        second_ref[k, l] = jnp.where(even, left, right)

    for k in range(2):
        for l in range(LAYERS):
            send(k, l, left_in[k, l], right_in[k, l])
    low_ref[0:2] = low_in[...]
    high_ref[0:2] = high_in[...]
    slot = iota((8, RUN), 1) // 4

    def stored(l):
        return pltpu.make_async_copy(field_ref.at[l], field_hbm.at[l], field_sem.at[l])

    def layer(l, _):
        sides = [jnp.zeros((8, RUN), F32) for _ in range(2)]
        for g in range(GROUPS):
            for h in range(2):
                cols = slice(h * RUN, (h + 1) * RUN)
                start = pl.multiple_of(l * 512 + g * 16 + h * 8, 8)
                terms = [acc[pl.ds(start, 8), :] for acc in accs]
                while len(terms) > 1:
                    terms = [sum(terms[i : i + 2]) for i in range(0, len(terms), 2)]
                total = terms[0]
                field_ref[l, 8 * g : 8 * g + 8, cols] = total
                if h == 0:
                    sides[0] = fold_left(sides[0], total, g, slot)
                else:
                    sides[1] = fold_right(sides[1], total, g, slot)
                if g == 0:
                    low_ref[2, l, :, cols] = total[:4]
                if g == GROUPS - 1:
                    high_ref[2, l, :, cols] = total[4:]
        send(2, l, sides[0], sides[1])
        stored(l).start()
        return 0

    lax.fori_loop(0, LAYERS, layer, 0)
    for l in range(LAYERS):
        stored(l).wait()


def gather(flags, incoming, left, right, low, high):
    vmem = pl.BlockSpec(memory_space=pltpu.VMEM)
    hbm = pl.BlockSpec(memory_space=pl.ANY)
    smem = pl.BlockSpec(memory_space=pltpu.SMEM)
    return pl.pallas_call(
        gather_kernel,
        out_shape=(
            jax.ShapeDtypeStruct((LAYERS, NX, NY), F32),
            jax.ShapeDtypeStruct((3, LAYERS, 8, RUN), F32),
            jax.ShapeDtypeStruct((3, LAYERS, 8, RUN), F32),
            jax.ShapeDtypeStruct((3, LAYERS, 4, NY), F32),
            jax.ShapeDtypeStruct((3, LAYERS, 4, NY), F32),
        ),
        in_specs=[smem, hbm] + [vmem] * 4,
        out_specs=(hbm,) + (vmem,) * 4,
        scratch_shapes=[
            pltpu.VMEM((128 * CHUNK, RUN), F32),
            pltpu.VMEM((LAYERS, NX, NY), F32),
            pltpu.VMEM((128, RUN), jnp.int32),
            pltpu.SMEM((128, RUN), jnp.int32),
            pltpu.SemaphoreType.DMA((8,)),
            pltpu.SemaphoreType.DMA,
            pltpu.SemaphoreType.DMA((LAYERS,)),
        ]
        + [pltpu.VMEM((POSITIONS + 8, RUN), F32)] * ACCS,
        compiler_params=pltpu.CompilerParams(vmem_limit_bytes=VMEM_LIMIT),
    )(flags, incoming, left, right, low, high)


def corner_kernel(flag_ref, first_in, second_in, low_in, high_in, first_ref, second_ref):
    slot = iota((8, RUN), 1) // 4
    even_y = flag_ref[4] > 0
    even_x = flag_ref[5] > 0

    def send(l, cols, low, high):
        first_ref[l, :, cols] = jnp.where(even_x, high, low)
        second_ref[l, :, cols] = jnp.where(even_x, low, high)

    for l in range(LAYERS):
        low = jnp.zeros((8, RUN), F32)
        high = jnp.zeros((8, RUN), F32)
        for q in range(3):
            a = first_in[q, l]
            b = second_in[q, l]
            for side in range(2):
                k = 2 * q + side
                v = jnp.where(even_y, a, b) if side else jnp.where(even_y, b, a)
                low = jnp.where(slot == k, pltpu.roll(v, (4 * k) % RUN, 1), low)
                high = jnp.where(slot == k, pltpu.roll(v, (4 * k + 4) % RUN, 1), high)
            send(l, slice(q * NY, (q + 1) * NY), low_in[q, l], high_in[q, l])
        send(l, slice(3 * NY, 3 * NY + RUN), low[:4], high[4:])


def corners(flags, first, second, low, high):
    smem = pl.BlockSpec(memory_space=pltpu.SMEM)
    vmem = pl.BlockSpec(memory_space=pltpu.VMEM)
    shape = jax.ShapeDtypeStruct((LAYERS, 4, 3 * NY + RUN), F32)
    return pl.pallas_call(
        corner_kernel,
        out_shape=(shape, shape),
        in_specs=[smem] + [vmem] * 4,
        out_specs=(vmem,) * 2,
    )(flags, first, second, low, high)


def sweep_kernel(
    kind_ref, slope_ref, flag_ref, warmth_hbm, q_hbm, field_hbm, first_y, second_y, first_x, second_x,
    out_hbm,
    warm_a, warm_b, q_ext, field_ext, r_row, f_row, g_row, shifted, sem,
):
    bodies = (warmth_hbm, q_hbm, field_hbm)
    exts = (warm_a, q_ext, field_ext)
    copies = []
    for k in range(3):
        for l in range(LAYERS):
            for h in range(2):
                copies.append(
                    pltpu.make_async_copy(
                        bodies[k].at[l, :, pl.ds(h * RUN, RUN)],
                        exts[k].at[l, h, pl.ds(BASE, NX), :],
                        sem.at[k, l, h],
                    )
                )
    for c in copies:
        c.start()
    has_left = flag_ref[0] > 0
    has_right = flag_ref[1] > 0
    has_low = flag_ref[2] > 0
    has_high = flag_ref[3] > 0
    even_y = flag_ref[4] > 0
    even_x = flag_ref[5] > 0
    fills = (0.0, WALL, 0.0)
    lane = iota((8, RUN), 1)
    first_half = lane < 64

    def halo(l, _):
        for k in range(3):
            a = first_y[k, l]
            b = second_y[k, l]
            v = jnp.where(has_left, jnp.where(even_y, b, a), fills[k])
            w = jnp.where(has_right, jnp.where(even_y, a, b), fills[k])
            v = pltpu.roll(v, RUN - 4, 1)
            for g in range(GROUPS):
                shift = (RUN - 4 * g) % RUN
                third = jnp.where(first_half, pltpu.roll(w, shift, 1), pltpu.roll(v, shift, 1))
                exts[k][l, 2, BASE + 8 * g : BASE + 8 * g + 8, :] = third
            for high, present, row in ((False, has_low, BASE - 4), (True, has_high, BASE + NX)):

                def received(cols):
                    a = first_x[l, :, cols]
                    b = second_x[l, :, cols]
                    return jnp.where(even_x, a, b) if high else jnp.where(even_x, b, a)

                for h in range(2):
                    main = received(slice(k * NY + h * RUN, k * NY + (h + 1) * RUN))
                    exts[k][l, h, row : row + 4, :] = jnp.where(present, main, fills[k])
                c = pltpu.roll(received(slice(3 * NY, 3 * NY + RUN)), RUN - (8 * k + 4), 1)
                cl = jnp.where(present & has_left, c, fills[k])
                cr = jnp.where(present & has_right, c, fills[k])
                exts[k][l, 2, row : row + 4, :] = jnp.where(first_half[:4], cr, cl)
        return 0

    lax.fori_loop(0, LAYERS, halo, 0)
    for c in copies:
        c.wait()

    last = lane == RUN - 1
    first = lane == 0

    def up(v):
        s = [pltpu.roll(x, RUN - 1, 1) for x in v]
        return [jnp.where(last, s[(h + 1) % 3], s[h]) for h in range(3)]

    def down(v):
        s = [pltpu.roll(x, 1, 1) for x in v]
        return [jnp.where(first, s[(h + 2) % 3], s[h]) for h in range(3)]

    def rcp(x):
        return pl.reciprocal(x, approx=True)

    slopes = [slope_ref[kind_ref[l]] for l in range(LAYERS)]

    def one_sweep(src, dst, top, stride):
        def load(ref, l, j):
            return [ref[l, h, pl.ds(top + j, 8, stride=stride), :] for h in range(3)]

        def resist(q, t, c):
            return [a * (1.0 + c * b) for a, b in zip(q, t)]

        def shift(l, r, t):
            for i, v in enumerate((up(r), down(r), up(t), down(t))):
                for h in range(3):
                    shifted[i, l, h] = v[h]

        for l in range(LAYERS):
            t0 = load(src, l, -1)
            t1 = load(src, l, 0)
            r0 = resist(load(q_ext, l, -1), t0, slopes[l])
            r1 = resist(load(q_ext, l, 0), t1, slopes[l])
            for h in range(3):
                g = rcp(r0[h] + r1[h])
                r_row[l, h] = r1[h]
                g_row[l, h] = g
                f_row[l, h] = g * (t1[h] - t0[h])
            shift(l, r1, t1)

        def step(j, _):
            fz = gz = None
            t = load(src, 0, j)
            r = [r_row[0, h] for h in range(3)]
            for l in range(LAYERS):
                tn = load(src, l, j + 1)
                rn = resist(load(q_ext, l, j + 1), tn, slopes[l])
                power = load(field_ext, l, j)
                if l < LAYERS - 1:
                    t_above = load(src, l + 1, j)
                    r_above = [r_row[l + 1, h] for h in range(3)]
                net = []
                den = []
                for h in range(3):
                    gx = rcp(r[h] + rn[h])
                    fx = gx * (tn[h] - t[h])
                    net.append(fx - f_row[l, h])
                    den.append(gx + g_row[l, h])
                    r_row[l, h] = rn[h]
                    f_row[l, h] = fx
                    g_row[l, h] = gx
                for h in range(3):
                    ru, rd, tu, td = (shifted[i, l, h] for i in range(4))
                    gu = rcp(r[h] + ru)
                    gd = rcp(r[h] + rd)
                    net[h] = net[h] + (gu * (tu - t[h]) + gd * (td - t[h]))
                    den[h] = den[h] + (gu + gd)
                shift(l, rn, tn)
                if l > 0:
                    for h in range(3):
                        net[h] = net[h] - fz[h]
                        den[h] = den[h] + gz[h]
                else:
                    for h in range(3):
                        net[h] = net[h] - 2.0 * t[h]
                        den[h] = den[h] + 2.0
                if l < LAYERS - 1:
                    gz = [0.5 * rcp(r[h] + r_above[h]) for h in range(3)]
                    fz = [gz[h] * (t_above[h] - t[h]) for h in range(3)]
                    for h in range(3):
                        net[h] = net[h] + fz[h]
                        den[h] = den[h] + gz[h]
                for h in range(3):
                    fresh = t[h] + (0.5 * power[h] + net[h]) * rcp(den[h])
                    dst[l, h, pl.ds(top + j, 8, stride=stride), :] = fresh
                if l < LAYERS - 1:
                    t = t_above
                    r = r_above
            return 0

        lax.fori_loop(0, stride, step, 0)

    one_sweep(warm_a, warm_b, BASE - 4, 33)
    one_sweep(warm_b, warm_a, BASE - 4, 33)
    one_sweep(warm_a, warm_b, BASE - 4, 33)
    copies = [
        pltpu.make_async_copy(
            warm_b.at[l, h, pl.ds(BASE, NX), :],
            out_hbm.at[l, :, pl.ds(h * RUN, RUN)],
            sem.at[0, l, h],
        )
        for l in range(LAYERS)
        for h in range(2)
    ]
    for c in copies:
        c.start()
    for c in copies:
        c.wait()


def sweeps(kind, slope, flags, warmth, q, field, first_y, second_y, first_x, second_x):
    vmem = pl.BlockSpec(memory_space=pltpu.VMEM)
    smem = pl.BlockSpec(memory_space=pltpu.SMEM)
    hbm = pl.BlockSpec(memory_space=pl.ANY)
    ext = pltpu.VMEM((LAYERS, 3, ROWS, RUN), F32)
    row = pltpu.VMEM((LAYERS, 3, 8, RUN), F32)
    return pl.pallas_call(
        sweep_kernel,
        out_shape=jax.ShapeDtypeStruct((LAYERS, NX, NY), F32),
        in_specs=[smem, smem, smem, hbm, hbm, hbm, vmem, vmem, vmem, vmem],
        out_specs=hbm,
        scratch_shapes=[
            ext,
            ext,
            ext,
            ext,
            row,
            row,
            row,
            pltpu.VMEM((4, LAYERS, 3, 8, RUN), F32),
            pltpu.SemaphoreType.DMA((3, LAYERS, 2)),
        ],
        compiler_params=pltpu.CompilerParams(vmem_limit_bytes=VMEM_LIMIT),
    )(kind, slope, flags, warmth, q, field, first_y, second_y, first_x, second_x)


def swap(axis, first, second):
    n = lax.axis_size(axis)
    pairs = [(i, i ^ 1) for i in range(n)]
    others = [(i, (((i + 1) ^ 1) - 1) % n) for i in range(n)]
    return lax.ppermute(first, axis, pairs), lax.ppermute(second, axis, others)


def per_device(
    segment_wattage_table,
    segment_target_tile,
    occupied_slot_tally,
    segment_tile_position,
    stratum_substance,
    substance_transport_base,
    substance_thermal_slope,
    thermal_scaling_factor,
    starting_warmth_excess,
):
    tiles = 128
    outgoing = pack(
        occupied_slot_tally,
        segment_target_tile.reshape(-1, RUN),
        segment_tile_position.reshape(-1, RUN),
        segment_wattage_table,
    )
    incoming = lax.all_to_all(
        outgoing.reshape(tiles, 1, CHUNK * RUN), ("gx", "gy"), split_axis=0, concat_axis=0, tiled=True
    ).reshape(tiles * CHUNK, RUN)
    q, left, right, low, high = prepare(
        stratum_substance, substance_transport_base, starting_warmth_excess, thermal_scaling_factor
    )
    i = lax.axis_index("gx")
    k = lax.axis_index("gy")
    flags = jnp.stack(
        [
            k > 0,
            k < lax.axis_size("gy") - 1,
            i > 0,
            i < lax.axis_size("gx") - 1,
            k % 2 == 0,
            i % 2 == 0,
        ]
    ).astype(jnp.int32)
    field, first, second, low, high = gather(flags, incoming, left, right, low, high)
    first_y, second_y = swap("gy", first, second)
    first, second = corners(flags, first_y, second_y, low, high)
    first_x, second_x = swap("gx", first, second)
    final = sweeps(
        stratum_substance,
        substance_thermal_slope,
        flags,
        starting_warmth_excess,
        q,
        field,
        first_y,
        second_y,
        first_x,
        second_x,
    )
    return field, final


def solution(mesh):
    return jax.shard_map(
        per_device,
        mesh=mesh,
        in_specs=(
            P(("gx", "gy"), None),
            P(("gx", "gy")),
            P(("gx", "gy")),
            P(("gx", "gy")),
            P(),
            P(),
            P(),
            P(None, "gx", "gy"),
            P(None, "gx", "gy"),
        ),
        out_specs=(P(None, "gx", "gy"), P(None, "gx", "gy")),
        check_vma=False,
    )
```

```python
import jax
import jax.numpy as jnp
from jax import lax
from jax.experimental import pallas as pl
from jax.experimental.pallas import tpu as pltpu
from jax.sharding import PartitionSpec as P

RUN = 128
SWEEPS = 3
CAP = 48
CHUNK = CAP + 1
LAYERS = 8
NX = 256
NY = 256
GROUPS = NX // 8
POSITIONS = LAYERS * NX * NY // RUN
ACCS = 6
WALL = 1e30
BASE = 16
ROWS = 280
VMEM_LIMIT = 60 * 1024 * 1024
F32 = jnp.float32
BF16 = jnp.bfloat16


def iota(shape, dim):
    return lax.broadcasted_iota(jnp.int32, shape, dim)


def pack_kernel(
    tally_ref, target_ref, place_ref, table_hbm, out_ref, table_ref, dest_v, dest_s, sem, table_sem
):
    load = pltpu.make_async_copy(table_hbm, table_ref, table_sem)
    load.start()
    tally = tally_ref[0]
    tiles = 128
    sub = iota((tiles, RUN), 0)
    lane = iota((1, RUN), 1)
    tri_row = iota((RUN, 2 * RUN), 0)
    tri_col = iota((RUN, 2 * RUN), 1)
    tri = jnp.where((tri_row <= tri_col) | (tri_col >= RUN), 1.0, 0.0).astype(BF16)

    def rank_group(g, carry):
        seen, placed = carry
        live = (lane + g * RUN) < tally
        tgt = target_ref[pl.ds(g, 1), :]
        match = sub == jnp.where(live, tgt, -1)
        onehot = jnp.where(match, 1.0, 0.0)
        run = jnp.dot(onehot.astype(BF16), tri, preferred_element_type=F32)
        rank = jnp.sum(jnp.where(match, seen + run[:, :RUN], 0.0), axis=0, keepdims=True)
        rank = rank.astype(jnp.int32) - 1
        dest_v[pl.ds(g, 1), :] = jnp.where(live, tgt * CHUNK + rank, CAP)
        spot = place_ref[pl.ds(g, 1), :]
        spot = (spot & ~15) | ((spot & 1) << 3) | ((spot >> 1) & 7)
        spot = spot + 1
        digits = jnp.where(sub < 64, spot & 63, spot >> 6)
        chosen = jnp.where((sub & 63) == rank, digits, 0).astype(F32)
        placed = placed + lax.dot_general(
            onehot.astype(BF16),
            chosen.astype(BF16),
            (((1,), (1,)), ((), ())),
            preferred_element_type=F32,
        )
        return seen + run[:, RUN:], placed

    zero = jnp.zeros((tiles, RUN), F32)
    seen, placed = lax.fori_loop(0, 32, rank_group, (zero, zero), unroll=32)
    placed = placed + 64.0 * pltpu.roll(placed, 64, 1)
    copy = pltpu.make_async_copy(dest_v, dest_s, sem)
    copy.start()
    copy.wait()

    load.wait()

    def move(g, _):
        for k in range(RUN):
            out_ref[pl.ds(dest_s[g, k], 1), :] = table_ref[pl.ds(g * RUN + k, 1), :]
        return 0

    lax.fori_loop(0, (tally + RUN - 1) // RUN, move, 0)
    for t in range(tiles):
        out_ref[t * CHUNK + CAP : t * CHUNK + CAP + 1, :] = placed[t : t + 1, :]


def pack(tally, target, place, table):
    tiles = 128
    return pl.pallas_call(
        pack_kernel,
        out_shape=jax.ShapeDtypeStruct((tiles * CHUNK, RUN), F32),
        in_specs=[
            pl.BlockSpec(memory_space=pltpu.SMEM),
            pl.BlockSpec(memory_space=pltpu.VMEM),
            pl.BlockSpec(memory_space=pltpu.VMEM),
            pl.BlockSpec(memory_space=pl.ANY),
        ],
        out_specs=pl.BlockSpec(memory_space=pltpu.VMEM),
        scratch_shapes=[
            pltpu.VMEM((32 * RUN, RUN), F32),
            pltpu.VMEM((32, RUN), jnp.int32),
            pltpu.SMEM((32, RUN), jnp.int32),
            pltpu.SemaphoreType.DMA,
            pltpu.SemaphoreType.DMA,
        ],
        compiler_params=pltpu.CompilerParams(vmem_limit_bytes=VMEM_LIMIT),
    )(tally, target, place, table)


def fold_left(kept, value, g, slot):
    return jnp.where(slot == g, pltpu.roll(value, (4 * g) % RUN, 1), kept)


def fold_right(kept, value, g, slot):
    return jnp.where(slot == g, pltpu.roll(value, (4 * g + 4) % RUN, 1), kept)


def prepare_kernel(
    kind_ref, base_ref, warmth_ref, scale_ref, q_ref, left_ref, right_ref, low_ref, high_ref
):
    slot = iota((8, RUN), 1) // 4

    def layer(l, _):
        inverse = 1.0 / jnp.full((8, RUN), base_ref[kind_ref[l]], F32)
        sides = [jnp.zeros((8, RUN), F32) for _ in range(4)]
        for g in range(GROUPS):
            for h in range(2):
                cols = slice(h * RUN, (h + 1) * RUN)
                t = warmth_ref[l, 8 * g : 8 * g + 8, cols]
                q = inverse / scale_ref[l, 8 * g : 8 * g + 8, cols]
                q_ref[l, 8 * g : 8 * g + 8, cols] = q
                if h == 0:
                    sides[0] = fold_left(sides[0], t, g, slot)
                    sides[1] = fold_left(sides[1], q, g, slot)
                else:
                    sides[2] = fold_right(sides[2], t, g, slot)
                    sides[3] = fold_right(sides[3], q, g, slot)
                if g == 0:
                    low_ref[0, l, :, cols] = t[:4]
                    low_ref[1, l, :, cols] = q[:4]
                if g == GROUPS - 1:
                    high_ref[0, l, :, cols] = t[4:]
                    high_ref[1, l, :, cols] = q[4:]
        left_ref[0, l] = sides[0]
        left_ref[1, l] = sides[1]
        right_ref[0, l] = sides[2]
        right_ref[1, l] = sides[3]
        return 0

    lax.fori_loop(0, LAYERS, layer, 0)


def prepare(kind, base, warmth, scale):
    vmem = pl.BlockSpec(memory_space=pltpu.VMEM)
    smem = pl.BlockSpec(memory_space=pltpu.SMEM)
    return pl.pallas_call(
        prepare_kernel,
        out_shape=(
            jax.ShapeDtypeStruct(warmth.shape, F32),
            jax.ShapeDtypeStruct((2, LAYERS, 8, RUN), F32),
            jax.ShapeDtypeStruct((2, LAYERS, 8, RUN), F32),
            jax.ShapeDtypeStruct((2, LAYERS, 4, NY), F32),
            jax.ShapeDtypeStruct((2, LAYERS, 4, NY), F32),
        ),
        in_specs=[smem, smem, vmem, vmem],
        out_specs=(vmem,) * 5,
        compiler_params=pltpu.CompilerParams(vmem_limit_bytes=16 * 1024 * 1024),
        cost_estimate=pl.CostEstimate(flops=8000000, bytes_accessed=6300000, transcendentals=0),
    )(kind, base, warmth, scale)


def gather_kernel(
    flag_ref, inc_ref, left_in, right_in, low_in, high_in,
    field_hbm, first_hbm, second_hbm, low_ref, high_ref,
    first_ref, second_ref, field_ref, spot_v, spot_s, spot_sem, field_sem, side_sem, *accs,
):
    tiles = 128
    for t in range(tiles):
        row = inc_ref[t * CHUNK + CAP : t * CHUNK + CAP + 1, :]
        spot_v[t : t + 1, :] = jnp.where(row > 0.5, row.astype(jnp.int32) - 1, POSITIONS)
    copy = pltpu.make_async_copy(spot_v, spot_s, spot_sem)
    copy.start()

    def clear(i, _):
        for acc in accs:
            acc[pl.ds(pl.multiple_of(i * 64, 64), 64), :] = jnp.zeros((64, RUN), F32)
        return 0

    lax.fori_loop(0, POSITIONS // 64, clear, 0)
    copy.wait()

    def source(s, _):
        for p in range(CAP):
            acc = accs[p % ACCS]
            acc[pl.ds(spot_s[s, p], 1), :] += inc_ref[pl.ds(s * CHUNK + p, 1), :]
        return 0

    lax.fori_loop(0, tiles, source, 0)
    even = flag_ref[4] > 0

    def send(k, l, left, right):
        first_ref[k, l] = jnp.where(even, right, left)
        second_ref[k, l] = jnp.where(even, left, right)

    for k in range(2):
        for l in range(LAYERS):
            send(k, l, left_in[k, l], right_in[k, l])
    low_ref[0:2] = low_in[...]
    high_ref[0:2] = high_in[...]
    slot = iota((8, RUN), 1) // 4

    def stored(l):
        return pltpu.make_async_copy(field_ref.at[l], field_hbm.at[l], field_sem.at[l])

    def layer(l, _):
        sides = [jnp.zeros((8, RUN), F32) for _ in range(2)]
        for g in range(GROUPS):
            for h in range(2):
                cols = slice(h * RUN, (h + 1) * RUN)
                start = pl.multiple_of(l * 512 + g * 16 + h * 8, 8)
                v = [acc[pl.ds(start, 8), :] for acc in accs]
                total = ((v[0] + v[1]) + (v[2] + v[3])) + (v[4] + v[5])
                field_ref[l, 8 * g : 8 * g + 8, cols] = total
                if h == 0:
                    sides[0] = fold_left(sides[0], total, g, slot)
                else:
                    sides[1] = fold_right(sides[1], total, g, slot)
                if g == 0:
                    low_ref[2, l, :, cols] = total[:4]
                if g == GROUPS - 1:
                    high_ref[2, l, :, cols] = total[4:]
        send(2, l, sides[0], sides[1])
        stored(l).start()
        return 0

    lax.fori_loop(0, LAYERS, layer, 0)
    sides = [
        pltpu.make_async_copy(first_ref, first_hbm, side_sem.at[0]),
        pltpu.make_async_copy(second_ref, second_hbm, side_sem.at[1]),
    ]
    for c in sides:
        c.start()
    for l in range(LAYERS):
        stored(l).wait()
    for c in sides:
        c.wait()


def gather(flags, incoming, left, right, low, high):
    vmem = pl.BlockSpec(memory_space=pltpu.VMEM)
    hbm = pl.BlockSpec(memory_space=pltpu.HBM)
    smem = pl.BlockSpec(memory_space=pltpu.SMEM)
    return pl.pallas_call(
        gather_kernel,
        out_shape=(
            jax.ShapeDtypeStruct((LAYERS, NX, NY), F32),
            jax.ShapeDtypeStruct((3, LAYERS, 8, RUN), F32),
            jax.ShapeDtypeStruct((3, LAYERS, 8, RUN), F32),
            jax.ShapeDtypeStruct((3, LAYERS, 4, NY), F32),
            jax.ShapeDtypeStruct((3, LAYERS, 4, NY), F32),
        ),
        in_specs=[smem] + [vmem] * 5,
        out_specs=(hbm,) * 3 + (vmem,) * 2,
        scratch_shapes=[
            pltpu.VMEM((3, LAYERS, 8, RUN), F32),
            pltpu.VMEM((3, LAYERS, 8, RUN), F32),
            pltpu.VMEM((LAYERS, NX, NY), F32),
            pltpu.VMEM((128, RUN), jnp.int32),
            pltpu.SMEM((128, RUN), jnp.int32),
            pltpu.SemaphoreType.DMA,
            pltpu.SemaphoreType.DMA((LAYERS,)),
            pltpu.SemaphoreType.DMA((2,)),
        ]
        + [pltpu.VMEM((POSITIONS + 8, RUN), F32)] * ACCS,
        compiler_params=pltpu.CompilerParams(vmem_limit_bytes=24 * 1024 * 1024),
    )(flags, incoming, left, right, low, high)


def corner_kernel(
    flag_ref, first_in, second_in, low_in, high_in, first_hbm, second_hbm, first_ref, second_ref, sem
):
    slot = iota((8, RUN), 1) // 4
    even_y = flag_ref[4] > 0
    even_x = flag_ref[5] > 0

    def send(l, cols, low, high):
        first_ref[l, :, cols] = jnp.where(even_x, high, low)
        second_ref[l, :, cols] = jnp.where(even_x, low, high)

    for l in range(LAYERS):
        low = jnp.zeros((8, RUN), F32)
        high = jnp.zeros((8, RUN), F32)
        for q in range(3):
            a = first_in[q, l]
            b = second_in[q, l]
            for side in range(2):
                k = 2 * q + side
                v = jnp.where(even_y, a, b) if side else jnp.where(even_y, b, a)
                low = jnp.where(slot == k, pltpu.roll(v, (4 * k) % RUN, 1), low)
                high = jnp.where(slot == k, pltpu.roll(v, (4 * k + 4) % RUN, 1), high)
            send(l, slice(q * NY, (q + 1) * NY), low_in[q, l], high_in[q, l])
        send(l, slice(3 * NY, 3 * NY + RUN), low[:4], high[4:])
    sides = [
        pltpu.make_async_copy(first_ref, first_hbm, sem.at[0]),
        pltpu.make_async_copy(second_ref, second_hbm, sem.at[1]),
    ]
    for c in sides:
        c.start()
    for c in sides:
        c.wait()


def corners(flags, first, second, low, high):
    smem = pl.BlockSpec(memory_space=pltpu.SMEM)
    vmem = pl.BlockSpec(memory_space=pltpu.VMEM)
    shape = jax.ShapeDtypeStruct((LAYERS, 4, 3 * NY + RUN), F32)
    return pl.pallas_call(
        corner_kernel,
        out_shape=(shape, shape),
        in_specs=[smem] + [vmem] * 4,
        out_specs=(pl.BlockSpec(memory_space=pltpu.HBM),) * 2,
        scratch_shapes=[pltpu.VMEM(shape.shape, F32)] * 2 + [pltpu.SemaphoreType.DMA((2,))],
        compiler_params=pltpu.CompilerParams(vmem_limit_bytes=4 * 1024 * 1024),
    )(flags, first, second, low, high)


def sweep_kernel(
    kind_ref, slope_ref, flag_ref, warmth_hbm, q_hbm, field_hbm, first_y, second_y, first_x, second_x,
    out_hbm,
    warm_a, warm_b, q_ext, field_ext, r_row, f_row, g_row, shifted, sem,
):
    bodies = (warmth_hbm, q_hbm, field_hbm)
    exts = (warm_a, q_ext, field_ext)
    copies = []
    for k in range(3):
        for l in range(LAYERS):
            for h in range(2):
                copies.append(
                    pltpu.make_async_copy(
                        bodies[k].at[l, :, pl.ds(h * RUN, RUN)],
                        exts[k].at[l, h, pl.ds(BASE, NX), :],
                        sem.at[k, l, h],
                    )
                )
    for c in copies:
        c.start()
    has_left = flag_ref[0] > 0
    has_right = flag_ref[1] > 0
    has_low = flag_ref[2] > 0
    has_high = flag_ref[3] > 0
    even_y = flag_ref[4] > 0
    even_x = flag_ref[5] > 0
    fills = (0.0, WALL, 0.0)
    lane = iota((8, RUN), 1)
    first_half = lane < 64

    def halo(l, _):
        for k in range(3):
            a = first_y[k, l]
            b = second_y[k, l]
            v = jnp.where(has_left, jnp.where(even_y, b, a), fills[k])
            w = jnp.where(has_right, jnp.where(even_y, a, b), fills[k])
            v = pltpu.roll(v, RUN - 4, 1)
            for g in range(GROUPS):
                shift = (RUN - 4 * g) % RUN
                third = jnp.where(first_half, pltpu.roll(w, shift, 1), pltpu.roll(v, shift, 1))
                exts[k][l, 2, BASE + 8 * g : BASE + 8 * g + 8, :] = third
            for high, present, row in ((False, has_low, BASE - 4), (True, has_high, BASE + NX)):

                def received(cols):
                    a = first_x[l, :, cols]
                    b = second_x[l, :, cols]
                    return jnp.where(even_x, a, b) if high else jnp.where(even_x, b, a)

                for h in range(2):
                    main = received(slice(k * NY + h * RUN, k * NY + (h + 1) * RUN))
                    exts[k][l, h, row : row + 4, :] = jnp.where(present, main, fills[k])
                c = pltpu.roll(received(slice(3 * NY, 3 * NY + RUN)), RUN - (8 * k + 4), 1)
                cl = jnp.where(present & has_left, c, fills[k])
                cr = jnp.where(present & has_right, c, fills[k])
                exts[k][l, 2, row : row + 4, :] = jnp.where(first_half[:4], cr, cl)
        return 0

    lax.fori_loop(0, LAYERS, halo, 0)
    for c in copies:
        c.wait()

    last = lane == RUN - 1
    first = lane == 0

    def up(v):
        s = [pltpu.roll(x, RUN - 1, 1) for x in v]
        return [jnp.where(last, s[(h + 1) % 3], s[h]) for h in range(3)]

    def down(v):
        s = [pltpu.roll(x, 1, 1) for x in v]
        return [jnp.where(first, s[(h + 2) % 3], s[h]) for h in range(3)]

    def rcp(x):
        return pl.reciprocal(x, approx=True)

    slopes = [slope_ref[kind_ref[l]] for l in range(LAYERS)]

    def one_sweep(src, dst, top, stride):
        def load(ref, l, j):
            return [ref[l, h, pl.ds(top + j, 8, stride=stride), :] for h in range(3)]

        def resist(q, t, c):
            return [a * (1.0 + c * b) for a, b in zip(q, t)]

        def shift(l, r, t):
            for i, v in enumerate((up(r), down(r), up(t), down(t))):
                for h in range(3):
                    shifted[i, l, h] = v[h]

        for l in range(LAYERS):
            t0 = load(src, l, -1)
            t1 = load(src, l, 0)
            r0 = resist(load(q_ext, l, -1), t0, slopes[l])
            r1 = resist(load(q_ext, l, 0), t1, slopes[l])
            for h in range(3):
                g = rcp(r0[h] + r1[h])
                r_row[l, h] = r1[h]
                g_row[l, h] = g
                f_row[l, h] = g * (t1[h] - t0[h])
            shift(l, r1, t1)

        def step(j, _):
            fz = gz = None
            t = load(src, 0, j)
            r = [r_row[0, h] for h in range(3)]
            for l in range(LAYERS):
                tn = load(src, l, j + 1)
                rn = resist(load(q_ext, l, j + 1), tn, slopes[l])
                power = load(field_ext, l, j)
                if l < LAYERS - 1:
                    t_above = load(src, l + 1, j)
                    r_above = [r_row[l + 1, h] for h in range(3)]
                net = []
                den = []
                for h in range(3):
                    gx = rcp(r[h] + rn[h])
                    fx = gx * (tn[h] - t[h])
                    net.append(fx - f_row[l, h])
                    den.append(gx + g_row[l, h])
                    r_row[l, h] = rn[h]
                    f_row[l, h] = fx
                    g_row[l, h] = gx
                for h in range(3):
                    ru, rd, tu, td = (shifted[i, l, h] for i in range(4))
                    gu = rcp(r[h] + ru)
                    gd = rcp(r[h] + rd)
                    net[h] = net[h] + (gu * (tu - t[h]) + gd * (td - t[h]))
                    den[h] = den[h] + (gu + gd)
                shift(l, rn, tn)
                if l > 0:
                    for h in range(3):
                        net[h] = net[h] - fz[h]
                        den[h] = den[h] + gz[h]
                else:
                    for h in range(3):
                        net[h] = net[h] - 2.0 * t[h]
                        den[h] = den[h] + 2.0
                if l < LAYERS - 1:
                    gz = [0.5 * rcp(r[h] + r_above[h]) for h in range(3)]
                    fz = [gz[h] * (t_above[h] - t[h]) for h in range(3)]
                    for h in range(3):
                        net[h] = net[h] + fz[h]
                        den[h] = den[h] + gz[h]
                for h in range(3):
                    fresh = t[h] + (0.5 * power[h] + net[h]) * rcp(den[h])
                    dst[l, h, pl.ds(top + j, 8, stride=stride), :] = fresh
                if l < LAYERS - 1:
                    t = t_above
                    r = r_above
            return 0

        lax.fori_loop(0, stride, step, 0)

    one_sweep(warm_a, warm_b, BASE - 4, 33)
    one_sweep(warm_b, warm_a, BASE - 4, 33)
    one_sweep(warm_a, warm_b, BASE - 4, 33)
    copies = [
        pltpu.make_async_copy(
            warm_b.at[l, h, pl.ds(BASE, NX), :],
            out_hbm.at[l, :, pl.ds(h * RUN, RUN)],
            sem.at[0, l, h],
        )
        for l in range(LAYERS)
        for h in range(2)
    ]
    for c in copies:
        c.start()
    for c in copies:
        c.wait()


def sweeps(kind, slope, flags, warmth, q, field, first_y, second_y, first_x, second_x):
    vmem = pl.BlockSpec(memory_space=pltpu.VMEM)
    smem = pl.BlockSpec(memory_space=pltpu.SMEM)
    hbm = pl.BlockSpec(memory_space=pltpu.HBM)
    ext = pltpu.VMEM((LAYERS, 3, ROWS, RUN), F32)
    row = pltpu.VMEM((LAYERS, 3, 8, RUN), F32)
    return pl.pallas_call(
        sweep_kernel,
        out_shape=jax.ShapeDtypeStruct((LAYERS, NX, NY), F32),
        in_specs=[smem, smem, smem, hbm, hbm, hbm, vmem, vmem, vmem, vmem],
        out_specs=hbm,
        scratch_shapes=[
            ext,
            ext,
            ext,
            ext,
            row,
            row,
            row,
            pltpu.VMEM((4, LAYERS, 3, 8, RUN), F32),
            pltpu.SemaphoreType.DMA((3, LAYERS, 2)),
        ],
        compiler_params=pltpu.CompilerParams(vmem_limit_bytes=64 * 1024 * 1024 - 1600 * 1024),
    )(kind, slope, flags, warmth, q, field, first_y, second_y, first_x, second_x)


def swap(axis, first, second):
    n = lax.axis_size(axis)
    pairs = [(i, i ^ 1) for i in range(n)]
    others = [(i, (((i + 1) ^ 1) - 1) % n) for i in range(n)]
    return lax.ppermute(first, axis, pairs), lax.ppermute(second, axis, others)


def per_device(
    segment_wattage_table,
    segment_target_tile,
    occupied_slot_tally,
    segment_tile_position,
    stratum_substance,
    substance_transport_base,
    substance_thermal_slope,
    thermal_scaling_factor,
    starting_warmth_excess,
):
    tiles = 128
    outgoing = pack(
        occupied_slot_tally,
        segment_target_tile.reshape(-1, RUN),
        segment_tile_position.reshape(-1, RUN),
        segment_wattage_table,
    )
    incoming = lax.all_to_all(
        outgoing.reshape(tiles, 1, CHUNK * RUN), ("gx", "gy"), split_axis=0, concat_axis=0, tiled=True
    ).reshape(tiles * CHUNK, RUN)
    q, left, right, low, high = prepare(
        stratum_substance, substance_transport_base, starting_warmth_excess, thermal_scaling_factor
    )
    i = lax.axis_index("gx")
    k = lax.axis_index("gy")
    flags = jnp.stack(
        [
            k > 0,
            k < lax.axis_size("gy") - 1,
            i > 0,
            i < lax.axis_size("gx") - 1,
            k % 2 == 0,
            i % 2 == 0,
        ]
    ).astype(jnp.int32)
    field, first, second, low, high = gather(flags, incoming, left, right, low, high)
    first_y, second_y = swap("gy", first, second)
    first, second = corners(flags, first_y, second_y, low, high)
    first_x, second_x = swap("gx", first, second)
    final = sweeps(
        stratum_substance,
        substance_thermal_slope,
        flags,
        starting_warmth_excess,
        q,
        field,
        first_y,
        second_y,
        first_x,
        second_x,
    )
    return field, final


def solution(mesh):
    return jax.shard_map(
        per_device,
        mesh=mesh,
        in_specs=(
            P(("gx", "gy"), None),
            P(("gx", "gy")),
            P(("gx", "gy")),
            P(("gx", "gy")),
            P(),
            P(),
            P(),
            P(None, "gx", "gy"),
            P(None, "gx", "gy"),
        ),
        out_specs=(P(None, "gx", "gy"), P(None, "gx", "gy")),
        check_vma=False,
    )
```

```python
import jax
import jax.numpy as jnp
from jax import lax
from jax.experimental import pallas as pl
from jax.experimental.pallas import tpu as pltpu
from jax.sharding import PartitionSpec as P

RUN = 128
SWEEPS = 3
CAP = 48
CHUNK = CAP + 1
LAYERS = 8
NX = 256
NY = 256
GROUPS = NX // 8
POSITIONS = LAYERS * NX * NY // RUN
ACCS = 6
FIELDS = ((0, 3), (3, 3), (6, 2))
WALL = 1e30
SINK = 4.0
BASE = 16
ROWS = 280
VMEM_LIMIT = 60 * 1024 * 1024
F32 = jnp.float32
BF16 = jnp.bfloat16


def iota(shape, dim):
    return lax.broadcasted_iota(jnp.int32, shape, dim)


def pack_kernel(
    tally_ref, target_ref, place_ref, table_hbm, out_ref, table_ref, dest_v, dest_s, sem, table_sem
):
    load = pltpu.make_async_copy(table_hbm, table_ref, table_sem)
    load.start()
    tally = tally_ref[0]
    tiles = 128
    sub = iota((tiles, RUN), 0)
    lane = iota((1, RUN), 1)
    tri_row = iota((RUN, 2 * RUN), 0)
    tri_col = iota((RUN, 2 * RUN), 1)
    tri = jnp.where((tri_row <= tri_col) | (tri_col >= RUN), 1.0, 0.0).astype(BF16)

    def rank_group(g, carry):
        seen, placed = carry
        live = (lane + g * RUN) < tally
        tgt = target_ref[pl.ds(g, 1), :]
        match = sub == jnp.where(live, tgt, -1)
        onehot = jnp.where(match, 1.0, 0.0)
        run = jnp.dot(onehot.astype(BF16), tri, preferred_element_type=F32)
        rank = jnp.sum(jnp.where(match, seen + run[:, :RUN], 0.0), axis=0, keepdims=True)
        rank = rank.astype(jnp.int32) - 1
        dest_v[pl.ds(g, 1), :] = jnp.where(live, tgt * CHUNK + rank, CAP)
        spot = place_ref[pl.ds(g, 1), :]
        spot = (spot & ~15) | ((spot & 1) << 3) | ((spot >> 1) & 7)
        spot = spot + 1
        digits = jnp.where(sub < 64, spot & 63, spot >> 6)
        chosen = jnp.where((sub & 63) == rank, digits, 0).astype(F32)
        placed = placed + lax.dot_general(
            onehot.astype(BF16),
            chosen.astype(BF16),
            (((1,), (1,)), ((), ())),
            preferred_element_type=F32,
        )
        return seen + run[:, RUN:], placed

    zero = jnp.zeros((tiles, RUN), F32)
    seen, placed = lax.fori_loop(0, 32, rank_group, (zero, zero), unroll=32)
    placed = placed + 64.0 * pltpu.roll(placed, 64, 1)
    copy = pltpu.make_async_copy(dest_v, dest_s, sem)
    copy.start()
    copy.wait()

    load.wait()

    def move(g, _):
        for k in range(RUN):
            out_ref[pl.ds(dest_s[g, k], 1), :] = table_ref[pl.ds(g * RUN + k, 1), :]
        return 0

    lax.fori_loop(0, (tally + RUN - 1) // RUN, move, 0)
    for t in range(tiles):
        out_ref[t * CHUNK + CAP : t * CHUNK + CAP + 1, :] = placed[t : t + 1, :]


def pack(tally, target, place, table):
    tiles = 128
    return pl.pallas_call(
        pack_kernel,
        out_shape=jax.ShapeDtypeStruct((tiles * CHUNK, RUN), F32),
        in_specs=[
            pl.BlockSpec(memory_space=pltpu.SMEM),
            pl.BlockSpec(memory_space=pltpu.VMEM),
            pl.BlockSpec(memory_space=pltpu.VMEM),
            pl.BlockSpec(memory_space=pl.ANY),
        ],
        out_specs=pl.BlockSpec(memory_space=pltpu.VMEM),
        scratch_shapes=[
            pltpu.VMEM((32 * RUN, RUN), F32),
            pltpu.VMEM((32, RUN), jnp.int32),
            pltpu.SMEM((32, RUN), jnp.int32),
            pltpu.SemaphoreType.DMA,
            pltpu.SemaphoreType.DMA,
        ],
        compiler_params=pltpu.CompilerParams(vmem_limit_bytes=VMEM_LIMIT),
    )(tally, target, place, table)


def fold(kept, value, shift, slot, g):
    return jnp.where(slot == g, pltpu.roll(value, shift % RUN, 1), kept)


def prepare_kernel(
    kind_ref, base_ref, slope_ref, warmth_ref, scale_ref, q_ref, left_ref, right_ref, low_ref, high_ref
):
    lane = iota((8, RUN), 1)
    slot = lane // 8
    use_q = lane % 8 >= 3
    sub = iota((8, RUN), 0)

    def layer(l, _):
        kind = kind_ref[l]
        ratio = jnp.full((8, RUN), 0.5 * slope_ref[kind], F32) / jnp.full((8, RUN), base_ref[kind], F32)
        zero = jnp.zeros((8, RUN), F32)
        left = [[zero, zero], [zero, zero]]
        right = [[zero, zero], [zero, zero]]
        for g in range(GROUPS):
            half = g // 16
            k = g % 16
            for h in range(2):
                cols = slice(h * RUN, (h + 1) * RUN)
                t = warmth_ref[l, 8 * g : 8 * g + 8, cols]
                q = ratio / scale_ref[l, 8 * g : 8 * g + 8, cols]
                q_ref[l, 8 * g : 8 * g + 8, cols] = q
                if h == 0:
                    left[half][0] = fold(left[half][0], t, 8 * k, slot, k)
                    left[half][1] = fold(left[half][1], q, 8 * k + 3, slot, k)
                else:
                    right[half][0] = fold(right[half][0], t, 8 * k + 3, slot, k)
                    right[half][1] = fold(right[half][1], q, 8 * k + 6, slot, k)
                if g == 0:
                    low_ref[l, :, cols] = jnp.where(sub < 3, t, pltpu.roll(q, 3, 0))
                if g == GROUPS - 1:
                    high_ref[l, :, cols] = jnp.where(sub < 3, pltpu.roll(t, 3, 0), pltpu.roll(q, 6, 0))
        for half in range(2):
            left_ref[l, half] = jnp.where(use_q, left[half][1], left[half][0])
            right_ref[l, half] = jnp.where(use_q, right[half][1], right[half][0])
        return 0

    lax.fori_loop(0, LAYERS, layer, 0)


def prepare(kind, base, slope, warmth, scale):
    vmem = pl.BlockSpec(memory_space=pltpu.VMEM)
    smem = pl.BlockSpec(memory_space=pltpu.SMEM)
    side = jax.ShapeDtypeStruct((LAYERS, 2, 8, RUN), F32)
    edge = jax.ShapeDtypeStruct((LAYERS, 8, NY), F32)
    return pl.pallas_call(
        prepare_kernel,
        out_shape=(jax.ShapeDtypeStruct(warmth.shape, F32), side, side, edge, edge),
        in_specs=[smem, smem, smem, vmem, vmem],
        out_specs=(vmem,) * 5,
        compiler_params=pltpu.CompilerParams(vmem_limit_bytes=16 * 1024 * 1024),
        cost_estimate=pl.CostEstimate(flops=8000000, bytes_accessed=6300000, transcendentals=0),
    )(kind, base, slope, warmth, scale)


def gather_kernel(
    flag_ref, inc_ref, left_in, right_in, low_in, high_in,
    field_hbm, first_hbm, second_hbm, low_ref, high_ref,
    first_ref, second_ref, field_ref, spot_v, spot_s, spot_sem, field_sem, side_sem, *accs,
):
    tiles = 128
    for t in range(tiles):
        row = inc_ref[t * CHUNK + CAP : t * CHUNK + CAP + 1, :]
        spot_v[t : t + 1, :] = jnp.where(row > 0.5, row.astype(jnp.int32) - 1, POSITIONS)
    copy = pltpu.make_async_copy(spot_v, spot_s, spot_sem)
    copy.start()

    def clear(i, _):
        for acc in accs:
            acc[pl.ds(pl.multiple_of(i * 64, 64), 64), :] = jnp.zeros((64, RUN), F32)
        return 0

    lax.fori_loop(0, POSITIONS // 64, clear, 0)
    copy.wait()

    def source(s, _):
        for p in range(CAP):
            acc = accs[p % ACCS]
            acc[pl.ds(spot_s[s, p], 1), :] += inc_ref[pl.ds(s * CHUNK + p, 1), :]
        return 0

    lax.fori_loop(0, tiles, source, 0)
    even = flag_ref[4] > 0
    lane = iota((8, RUN), 1)
    slot = lane // 8
    use_p = lane % 8 >= 6
    sub = iota((8, RUN), 0)

    def stored(l):
        return pltpu.make_async_copy(field_ref.at[l], field_hbm.at[l], field_sem.at[l])

    def layer(l, _):
        zero = jnp.zeros((8, RUN), F32)
        left = [zero, zero]
        right = [zero, zero]
        for g in range(GROUPS):
            half = g // 16
            k = g % 16
            for h in range(2):
                cols = slice(h * RUN, (h + 1) * RUN)
                start = pl.multiple_of(l * 512 + g * 16 + h * 8, 8)
                v = [acc[pl.ds(start, 8), :] for acc in accs]
                total = ((v[0] + v[1]) + (v[2] + v[3])) + (v[4] + v[5])
                field_ref[l, 8 * g : 8 * g + 8, cols] = total
                if h == 0:
                    left[half] = fold(left[half], total, 8 * k + 6, slot, k)
                else:
                    right[half] = fold(right[half], total, 8 * k + 8, slot, k)
                if g == 0:
                    low_ref[l, :, cols] = jnp.where(sub < 6, low_in[l, :, cols], pltpu.roll(total, 6, 0))
                if g == GROUPS - 1:
                    high_ref[l, :, cols] = jnp.where(sub < 6, high_in[l, :, cols], total)
        for half in range(2):
            lhs = jnp.where(use_p, left[half], left_in[l, half])
            rhs = jnp.where(use_p, right[half], right_in[l, half])
            first_ref[l, half] = jnp.where(even, rhs, lhs)
            second_ref[l, half] = jnp.where(even, lhs, rhs)
        stored(l).start()
        return 0

    lax.fori_loop(0, LAYERS, layer, 0)
    sides = [
        pltpu.make_async_copy(first_ref, first_hbm, side_sem.at[0]),
        pltpu.make_async_copy(second_ref, second_hbm, side_sem.at[1]),
    ]
    for c in sides:
        c.start()
    for l in range(LAYERS):
        stored(l).wait()
    for c in sides:
        c.wait()


def gather(flags, incoming, left, right, low, high):
    vmem = pl.BlockSpec(memory_space=pltpu.VMEM)
    hbm = pl.BlockSpec(memory_space=pltpu.HBM)
    smem = pl.BlockSpec(memory_space=pltpu.SMEM)
    return pl.pallas_call(
        gather_kernel,
        out_shape=(
            jax.ShapeDtypeStruct((LAYERS, NX, NY), F32),
            jax.ShapeDtypeStruct((LAYERS, 2, 8, RUN), F32),
            jax.ShapeDtypeStruct((LAYERS, 2, 8, RUN), F32),
            jax.ShapeDtypeStruct((LAYERS, 8, NY), F32),
            jax.ShapeDtypeStruct((LAYERS, 8, NY), F32),
        ),
        in_specs=[smem] + [vmem] * 5,
        out_specs=(hbm,) * 3 + (vmem,) * 2,
        scratch_shapes=[
            pltpu.VMEM((LAYERS, 2, 8, RUN), F32),
            pltpu.VMEM((LAYERS, 2, 8, RUN), F32),
            pltpu.VMEM((LAYERS, NX, NY), F32),
            pltpu.VMEM((128, RUN), jnp.int32),
            pltpu.SMEM((128, RUN), jnp.int32),
            pltpu.SemaphoreType.DMA,
            pltpu.SemaphoreType.DMA((LAYERS,)),
            pltpu.SemaphoreType.DMA((2,)),
        ]
        + [pltpu.VMEM((POSITIONS + 8, RUN), F32)] * ACCS,
        compiler_params=pltpu.CompilerParams(vmem_limit_bytes=24 * 1024 * 1024),
    )(flags, incoming, left, right, low, high)


def corner_kernel(
    flag_ref, first_in, second_in, low_in, high_in, first_hbm, second_hbm, first_ref, second_ref, sem
):
    even_y = flag_ref[4] > 0
    even_x = flag_ref[5] > 0

    def send(l, h, low, high):
        first_ref[l, h] = jnp.where(even_x, high, low)
        second_ref[l, h] = jnp.where(even_x, low, high)

    lane = iota((8, RUN), 1)
    low = jnp.zeros((8, RUN), F32)
    high = jnp.zeros((8, RUN), F32)
    for l in range(LAYERS):
        for h in range(2):
            cols = slice(h * RUN, (h + 1) * RUN)
            send(l, h, low_in[l, :, cols], high_in[l, :, cols])
        for start, width in FIELDS:
            for side in range(2):
                place = 16 * l + 2 * start + side * width
                chosen = (lane >= place) & (lane < place + width)
                for half in range(2):
                    a = first_in[l, half]
                    b = second_in[l, half]
                    v = jnp.where(even_y, a, b) if side else jnp.where(even_y, b, a)
                    if half == 0:
                        low = jnp.where(chosen, pltpu.roll(v, (place - start) % RUN, 1), low)
                    else:
                        high = jnp.where(chosen, pltpu.roll(v, (place - start - 120) % RUN, 1), high)
    send(LAYERS, 0, low, high)
    sides = [
        pltpu.make_async_copy(first_ref, first_hbm, sem.at[0]),
        pltpu.make_async_copy(second_ref, second_hbm, sem.at[1]),
    ]
    for c in sides:
        c.start()
    for c in sides:
        c.wait()


def corners(flags, first, second, low, high):
    smem = pl.BlockSpec(memory_space=pltpu.SMEM)
    vmem = pl.BlockSpec(memory_space=pltpu.VMEM)
    shape = jax.ShapeDtypeStruct((LAYERS + 1, 2, 8, RUN), F32)
    return pl.pallas_call(
        corner_kernel,
        out_shape=(shape, shape),
        in_specs=[smem] + [vmem] * 4,
        out_specs=(pl.BlockSpec(memory_space=pltpu.HBM),) * 2,
        scratch_shapes=[pltpu.VMEM(shape.shape, F32)] * 2 + [pltpu.SemaphoreType.DMA((2,))],
        compiler_params=pltpu.CompilerParams(vmem_limit_bytes=4 * 1024 * 1024),
    )(flags, first, second, low, high)


def sweep_kernel(
    kind_ref, slope_ref, flag_ref, warmth_hbm, q_hbm, field_hbm, first_y, second_y, first_x, second_x,
    out_hbm,
    warm_a, warm_b, q_ext, field_ext, q_up, q_down, r_next, f_below, g_below, inv_row, sem,
):
    bodies = (warmth_hbm, q_hbm, field_hbm)
    exts = (warm_a, q_ext, field_ext)
    def arriving(k, l):
        return [
            pltpu.make_async_copy(
                bodies[k].at[l, :, pl.ds(h * RUN, RUN)],
                exts[k].at[l, h, pl.ds(BASE, NX), :],
                sem.at[k, l, h],
            )
            for h in range(2)
        ]

    def leaving(l):
        return [
            pltpu.make_async_copy(
                warm_b.at[l, h, pl.ds(BASE, NX), :],
                out_hbm.at[l, :, pl.ds(h * RUN, RUN)],
                sem.at[0, l, h],
            )
            for h in range(2)
        ]

    for l in range(LAYERS):
        for k in range(3):
            for c in arriving(k, l):
                c.start()
    has_left = flag_ref[0] > 0
    has_right = flag_ref[1] > 0
    has_low = flag_ref[2] > 0
    has_high = flag_ref[3] > 0
    even_y = flag_ref[4] > 0
    even_x = flag_ref[5] > 0
    fills = (0.0, WALL, 0.0)
    lane = iota((8, RUN), 1)
    sub = iota((8, RUN), 0)
    first_half = lane < 64

    def halo(l):
        def received(high, h, l):
            a = first_x[l, h]
            b = second_x[l, h]
            return jnp.where(even_x, a, b) if high else jnp.where(even_x, b, a)

        for k, (start, width) in enumerate(FIELDS):
            pick = (lane + 8 - start) % 8 < 4
            for half in range(2):
                a = first_y[l, half]
                b = second_y[l, half]
                v = jnp.where(has_left, jnp.where(even_y, b, a), fills[k])
                w = jnp.where(has_right, jnp.where(even_y, a, b), fills[k])
                both = jnp.where(pick, w, pltpu.roll(v, RUN - width, 1))
                for g in range(16):
                    row = BASE + 8 * (16 * half + g)
                    shift = (RUN - 8 * g - start) % RUN
                    exts[k][l, 2, row : row + 8, :] = pltpu.roll(both, shift, 1)
            for high, present, row in (
                (False, has_low, BASE - width),
                (True, has_high, BASE + NX),
            ):
                for h in range(2):
                    main = jnp.where(present, received(high, h, l), fills[k])
                    exts[k][l, h, row : row + width, :] = main[start : start + width]
                c = received(high, 0, LAYERS)
                c = pltpu.roll(c, RUN - (16 * l + 2 * start + width), 1)
                cl = jnp.where(present & has_left, c, fills[k])
                cr = jnp.where(present & has_right, c, fills[k])
                c = jnp.where(first_half, cr, cl)
                top = 0 if high else 8 - width
                exts[k][l, 2, row : row + width, :] = c[top : top + width]

    last = lane == RUN - 1
    first = lane == 0

    def up(v):
        s = [pltpu.roll(x, RUN - 1, 1) for x in v]
        return [jnp.where(last, s[(h + 1) % 3], s[h]) for h in range(3)]

    def down(v):
        s = [pltpu.roll(x, 1, 1) for x in v]
        return [jnp.where(first, s[(h + 2) % 3], s[h]) for h in range(3)]

    def rcp(x):
        return pl.reciprocal(x, approx=True)

    inverse = [1.0 / jnp.full((8, RUN), slope_ref[kind_ref[l]], F32) for l in range(LAYERS)]
    for l in range(LAYERS):
        inv_row[l] = inverse[l]
    top = BASE - 4
    stride = 33

    def at(j):
        return pl.ds(top + j, 8, stride=stride)

    def load(ref, l, j):
        return [ref[l, h, at(j), :] for h in range(3)]

    def one_sweep(src, dst, opening, blocks):
        every = range(blocks)

        def resist(l, j, t):
            inv = inv_row[l]
            q = load(q_ext, l, j)
            return [q[h] * (t[h] + inv) for h in every]

        def arrive(l):
            for k in range(3):
                for c in arriving(k, l):
                    c.wait()
            halo(l)

        if opening:
            arrive(0)
        for l in range(LAYERS):
            above = l < LAYERS - 1
            if opening and above:
                arrive(l + 1)
            inv = inv_row[l]

            def own(j, t):
                return [r_next[j, h] for h in every] if l > 0 else resist(l, j, t)

            def beside(j, t):
                tu, td = up(t), down(t)
                if opening:
                    q = load(q_ext, l, j)
                    qu, qd = up(q), down(q)
                    for h in range(3):
                        q_up[l, h, at(j), :] = qu[h]
                        q_down[l, h, at(j), :] = qd[h]
                else:
                    qu, qd = load(q_up, l, j), load(q_down, l, j)
                ru = [qu[h] * (tu[h] + inv) for h in every]
                rd = [qd[h] * (td[h] + inv) for h in every]
                return tu, td, ru, rd

            before = load(src, l, -1)
            t = load(src, l, 0)
            r = own(0, t)
            rb = resist(l, -1, before)
            gx = [rcp(rb[h] + r[h]) for h in every]
            px = [gx[h] * before[h] for h in every]
            for j in range(stride):
                tu, td, ru, rd = beside(j, t)
                tn = load(src, l, j + 1)
                rn = own(j + 1, tn)
                if above:
                    ta = load(src, l + 1, j)
                    ra = resist(l + 1, j, ta)
                for h in every:
                    gu = rcp(r[h] + ru[h])
                    gd = rcp(r[h] + rd[h])
                    g = rcp(r[h] + rn[h])
                    numer = field_ext[l, h, at(j), :] + px[h]
                    numer = (numer + g * tn[h]) + (gu * tu[h] + gd * td[h])
                    denom = (g + gx[h]) + (gu + gd)
                    gx[h] = g
                    px[h] = g * t[h]
                    if l > 0:
                        numer = numer + f_below[j, h]
                        denom = denom + g_below[j, h]
                    else:
                        denom = denom + SINK
                    if above:
                        gz = 0.5 * rcp(r[h] + ra[h])
                        numer = numer + gz * ta[h]
                        denom = denom + gz
                        r_next[j, h] = ra[h]
                        g_below[j, h] = gz
                        f_below[j, h] = gz * t[h]
                    dst[l, h, at(j), :] = numer * rcp(denom)
                t = tn
                r = rn
            if above:
                ra = resist(l + 1, stride, load(src, l + 1, stride))
                for h in every:
                    r_next[stride, h] = ra[h]
            if dst is warm_b and not opening:
                for c in leaving(l):
                    c.start()

    one_sweep(warm_a, warm_b, True, 3)
    one_sweep(warm_b, warm_a, False, 3)
    one_sweep(warm_a, warm_b, False, 2)
    for l in range(LAYERS):
        for c in leaving(l):
            c.wait()


def sweeps(kind, slope, flags, warmth, q, field, first_y, second_y, first_x, second_x):
    vmem = pl.BlockSpec(memory_space=pltpu.VMEM)
    smem = pl.BlockSpec(memory_space=pltpu.SMEM)
    hbm = pl.BlockSpec(memory_space=pltpu.HBM)
    ext = pltpu.VMEM((LAYERS, 3, ROWS, RUN), F32)
    row = pltpu.VMEM((34, 3, 8, RUN), F32)
    return pl.pallas_call(
        sweep_kernel,
        out_shape=jax.ShapeDtypeStruct((LAYERS, NX, NY), F32),
        in_specs=[smem, smem, smem, hbm, hbm, hbm, vmem, vmem, vmem, vmem],
        out_specs=hbm,
        scratch_shapes=[
            ext,
            ext,
            ext,
            ext,
            ext,
            ext,
            row,
            row,
            row,
            pltpu.VMEM((LAYERS, 8, RUN), F32),
            pltpu.SemaphoreType.DMA((3, LAYERS, 2)),
        ],
        compiler_params=pltpu.CompilerParams(vmem_limit_bytes=64 * 1024 * 1024 - 1600 * 1024),
    )(kind, slope, flags, warmth, q, field, first_y, second_y, first_x, second_x)


def swap(axis, first, second):
    n = lax.axis_size(axis)
    pairs = [(i, i ^ 1) for i in range(n)]
    others = [(i, (((i + 1) ^ 1) - 1) % n) for i in range(n)]
    return lax.ppermute(first, axis, pairs), lax.ppermute(second, axis, others)


def per_device(
    segment_wattage_table,
    segment_target_tile,
    occupied_slot_tally,
    segment_tile_position,
    stratum_substance,
    substance_transport_base,
    substance_thermal_slope,
    thermal_scaling_factor,
    starting_warmth_excess,
):
    tiles = 128
    outgoing = pack(
        occupied_slot_tally,
        segment_target_tile.reshape(-1, RUN),
        segment_tile_position.reshape(-1, RUN),
        segment_wattage_table,
    )
    incoming = lax.all_to_all(
        outgoing.reshape(tiles, 1, CHUNK * RUN), ("gx", "gy"), split_axis=0, concat_axis=0, tiled=True
    ).reshape(tiles * CHUNK, RUN)
    q, left, right, low, high = prepare(
        stratum_substance,
        substance_transport_base,
        substance_thermal_slope,
        starting_warmth_excess,
        thermal_scaling_factor,
    )
    i = lax.axis_index("gx")
    k = lax.axis_index("gy")
    flags = jnp.stack(
        [
            k > 0,
            k < lax.axis_size("gy") - 1,
            i > 0,
            i < lax.axis_size("gx") - 1,
            k % 2 == 0,
            i % 2 == 0,
        ]
    ).astype(jnp.int32)
    field, first, second, low, high = gather(flags, incoming, left, right, low, high)
    first_y, second_y = swap("gy", first, second)
    first, second = corners(flags, first_y, second_y, low, high)
    first_x, second_x = swap("gx", first, second)
    final = sweeps(
        stratum_substance,
        substance_thermal_slope,
        flags,
        starting_warmth_excess,
        q,
        field,
        first_y,
        second_y,
        first_x,
        second_x,
    )
    return field, final


def solution(mesh):
    return jax.shard_map(
        per_device,
        mesh=mesh,
        in_specs=(
            P(("gx", "gy"), None),
            P(("gx", "gy")),
            P(("gx", "gy")),
            P(("gx", "gy")),
            P(),
            P(),
            P(),
            P(None, "gx", "gy"),
            P(None, "gx", "gy"),
        ),
        out_specs=(P(None, "gx", "gy"), P(None, "gx", "gy")),
        check_vma=False,
    )
```

```python
import jax
import jax.numpy as jnp
from jax import lax
from jax.experimental import pallas as pl
from jax.experimental.pallas import tpu as pltpu
from jax.sharding import PartitionSpec as P

RUN = 128
SWEEPS = 3
CAP = 48
CHUNK = CAP + 1
LAYERS = 8
NX = 256
NY = 256
GROUPS = NX // 8
POSITIONS = LAYERS * NX * NY // RUN
ACCS = 6
FIELDS = ((0, 3), (3, 3), (6, 2))
WALL = 1e30
SINK = 4.0
BASE = 16
ROWS = 280
VMEM_LIMIT = 60 * 1024 * 1024
F32 = jnp.float32
BF16 = jnp.bfloat16


def iota(shape, dim):
    return lax.broadcasted_iota(jnp.int32, shape, dim)


def pack_kernel(
    tally_ref, target_ref, place_ref, table_hbm, out_ref, table_ref, dest_v, dest_s, sem, table_sem
):
    load = pltpu.make_async_copy(table_hbm, table_ref, table_sem)
    load.start()
    tally = tally_ref[0]
    tiles = 128
    sub = iota((tiles, RUN), 0)
    lane = iota((1, RUN), 1)
    tri_row = iota((RUN, 2 * RUN), 0)
    tri_col = iota((RUN, 2 * RUN), 1)
    tri = jnp.where((tri_row <= tri_col) | (tri_col >= RUN), 1.0, 0.0).astype(BF16)

    def rank_group(g, carry):
        seen, placed = carry
        live = (lane + g * RUN) < tally
        tgt = target_ref[pl.ds(g, 1), :]
        match = sub == jnp.where(live, tgt, -1)
        onehot = jnp.where(match, 1.0, 0.0)
        run = jnp.dot(onehot.astype(BF16), tri, preferred_element_type=F32)
        rank = jnp.sum(jnp.where(match, seen + run[:, :RUN], 0.0), axis=0, keepdims=True)
        rank = rank.astype(jnp.int32) - 1
        dest_v[pl.ds(g, 1), :] = jnp.where(live, tgt * CHUNK + rank, CAP)
        spot = place_ref[pl.ds(g, 1), :]
        spot = (spot & ~15) | ((spot & 1) << 3) | ((spot >> 1) & 7)
        spot = spot + 1
        digits = jnp.where(sub < 64, spot & 63, spot >> 6)
        chosen = jnp.where((sub & 63) == rank, digits, 0).astype(F32)
        placed = placed + lax.dot_general(
            onehot.astype(BF16),
            chosen.astype(BF16),
            (((1,), (1,)), ((), ())),
            preferred_element_type=F32,
        )
        return seen + run[:, RUN:], placed

    zero = jnp.zeros((tiles, RUN), F32)
    seen, placed = lax.fori_loop(0, 32, rank_group, (zero, zero), unroll=32)
    placed = placed + 64.0 * pltpu.roll(placed, 64, 1)
    copy = pltpu.make_async_copy(dest_v, dest_s, sem)
    copy.start()
    copy.wait()

    load.wait()

    def move(g, _):
        for k in range(RUN):
            out_ref[pl.ds(dest_s[g, k], 1), :] = table_ref[pl.ds(g * RUN + k, 1), :]
        return 0

    lax.fori_loop(0, (tally + RUN - 1) // RUN, move, 0)
    for t in range(tiles):
        out_ref[t * CHUNK + CAP : t * CHUNK + CAP + 1, :] = placed[t : t + 1, :]


def pack(tally, target, place, table):
    tiles = 128
    return pl.pallas_call(
        pack_kernel,
        out_shape=jax.ShapeDtypeStruct((tiles * CHUNK, RUN), F32),
        in_specs=[
            pl.BlockSpec(memory_space=pltpu.SMEM),
            pl.BlockSpec(memory_space=pltpu.VMEM),
            pl.BlockSpec(memory_space=pltpu.VMEM),
            pl.BlockSpec(memory_space=pl.ANY),
        ],
        out_specs=pl.BlockSpec(memory_space=pltpu.VMEM),
        scratch_shapes=[
            pltpu.VMEM((32 * RUN, RUN), F32),
            pltpu.VMEM((32, RUN), jnp.int32),
            pltpu.SMEM((32, RUN), jnp.int32),
            pltpu.SemaphoreType.DMA,
            pltpu.SemaphoreType.DMA,
        ],
        compiler_params=pltpu.CompilerParams(vmem_limit_bytes=VMEM_LIMIT),
    )(tally, target, place, table)


def fold(kept, value, shift, slot, g):
    return jnp.where(slot == g, pltpu.roll(value, shift % RUN, 1), kept)


def prepare_kernel(
    kind_ref, base_ref, slope_ref, warmth_ref, scale_ref, q_ref, left_ref, right_ref, low_ref, high_ref
):
    lane = iota((8, RUN), 1)
    slot = lane // 8
    use_q = lane % 8 >= 3
    sub = iota((8, RUN), 0)

    def layer(l, _):
        kind = kind_ref[l]
        ratio = jnp.full((8, RUN), 0.5 * slope_ref[kind], F32) / jnp.full((8, RUN), base_ref[kind], F32)
        zero = jnp.zeros((8, RUN), F32)
        left = [[zero, zero], [zero, zero]]
        right = [[zero, zero], [zero, zero]]
        for g in range(GROUPS):
            half = g // 16
            k = g % 16
            for h in range(2):
                cols = slice(h * RUN, (h + 1) * RUN)
                t = warmth_ref[l, 8 * g : 8 * g + 8, cols]
                q = ratio / scale_ref[l, 8 * g : 8 * g + 8, cols]
                q_ref[l, 8 * g : 8 * g + 8, cols] = q
                if h == 0:
                    left[half][0] = fold(left[half][0], t, 8 * k, slot, k)
                    left[half][1] = fold(left[half][1], q, 8 * k + 3, slot, k)
                else:
                    right[half][0] = fold(right[half][0], t, 8 * k + 3, slot, k)
                    right[half][1] = fold(right[half][1], q, 8 * k + 6, slot, k)
                if g == 0:
                    low_ref[l, :, cols] = jnp.where(sub < 3, t, pltpu.roll(q, 3, 0))
                if g == GROUPS - 1:
                    high_ref[l, :, cols] = jnp.where(sub < 3, pltpu.roll(t, 3, 0), pltpu.roll(q, 6, 0))
        for half in range(2):
            left_ref[l, half] = jnp.where(use_q, left[half][1], left[half][0])
            right_ref[l, half] = jnp.where(use_q, right[half][1], right[half][0])
        return 0

    lax.fori_loop(0, LAYERS, layer, 0)


def prepare(kind, base, slope, warmth, scale):
    vmem = pl.BlockSpec(memory_space=pltpu.VMEM)
    smem = pl.BlockSpec(memory_space=pltpu.SMEM)
    side = jax.ShapeDtypeStruct((LAYERS, 2, 8, RUN), F32)
    edge = jax.ShapeDtypeStruct((LAYERS, 8, NY), F32)
    return pl.pallas_call(
        prepare_kernel,
        out_shape=(jax.ShapeDtypeStruct(warmth.shape, F32), side, side, edge, edge),
        in_specs=[smem, smem, smem, vmem, vmem],
        out_specs=(vmem,) * 5,
        compiler_params=pltpu.CompilerParams(vmem_limit_bytes=16 * 1024 * 1024),
        cost_estimate=pl.CostEstimate(flops=8000000, bytes_accessed=6300000, transcendentals=0),
    )(kind, base, slope, warmth, scale)


def gather_kernel(
    flag_ref, inc_ref, left_in, right_in, low_in, high_in,
    field_hbm, first_hbm, second_hbm, low_ref, high_ref,
    first_ref, second_ref, field_ref, spot_v, spot_s, spot_sem, field_sem, side_sem, *accs,
):
    tiles = 128
    for t in range(tiles):
        row = inc_ref[t * CHUNK + CAP : t * CHUNK + CAP + 1, :]
        spot_v[t : t + 1, :] = jnp.where(row > 0.5, row.astype(jnp.int32) - 1, POSITIONS)
    copy = pltpu.make_async_copy(spot_v, spot_s, spot_sem)
    copy.start()

    def clear(i, _):
        for acc in accs:
            acc[pl.ds(pl.multiple_of(i * 64, 64), 64), :] = jnp.zeros((64, RUN), F32)
        return 0

    lax.fori_loop(0, POSITIONS // 64, clear, 0)
    copy.wait()

    def source(s, _):
        for p in range(CAP):
            acc = accs[p % ACCS]
            acc[pl.ds(spot_s[s, p], 1), :] += inc_ref[pl.ds(s * CHUNK + p, 1), :]
        return 0

    lax.fori_loop(0, tiles, source, 0, unroll=4)
    even = flag_ref[4] > 0
    lane = iota((8, RUN), 1)
    slot = lane // 8
    use_p = lane % 8 >= 6
    sub = iota((8, RUN), 0)

    def stored(l):
        return pltpu.make_async_copy(field_ref.at[l], field_hbm.at[l], field_sem.at[l])

    def layer(l, _):
        zero = jnp.zeros((8, RUN), F32)
        left = [zero, zero]
        right = [zero, zero]
        for g in range(GROUPS):
            half = g // 16
            k = g % 16
            for h in range(2):
                cols = slice(h * RUN, (h + 1) * RUN)
                start = pl.multiple_of(l * 512 + g * 16 + h * 8, 8)
                v = [acc[pl.ds(start, 8), :] for acc in accs]
                total = ((v[0] + v[1]) + (v[2] + v[3])) + (v[4] + v[5])
                field_ref[l, 8 * g : 8 * g + 8, cols] = total
                if h == 0:
                    left[half] = fold(left[half], total, 8 * k + 6, slot, k)
                else:
                    right[half] = fold(right[half], total, 8 * k + 8, slot, k)
                if g == 0:
                    low_ref[l, :, cols] = jnp.where(sub < 6, low_in[l, :, cols], pltpu.roll(total, 6, 0))
                if g == GROUPS - 1:
                    high_ref[l, :, cols] = jnp.where(sub < 6, high_in[l, :, cols], total)
        for half in range(2):
            lhs = jnp.where(use_p, left[half], left_in[l, half])
            rhs = jnp.where(use_p, right[half], right_in[l, half])
            first_ref[l, half] = jnp.where(even, rhs, lhs)
            second_ref[l, half] = jnp.where(even, lhs, rhs)
        stored(l).start()
        return 0

    lax.fori_loop(0, LAYERS, layer, 0)
    sides = [
        pltpu.make_async_copy(first_ref, first_hbm, side_sem.at[0]),
        pltpu.make_async_copy(second_ref, second_hbm, side_sem.at[1]),
    ]
    for c in sides:
        c.start()
    for l in range(LAYERS):
        stored(l).wait()
    for c in sides:
        c.wait()


def gather(flags, incoming, left, right, low, high):
    vmem = pl.BlockSpec(memory_space=pltpu.VMEM)
    hbm = pl.BlockSpec(memory_space=pltpu.HBM)
    smem = pl.BlockSpec(memory_space=pltpu.SMEM)
    return pl.pallas_call(
        gather_kernel,
        out_shape=(
            jax.ShapeDtypeStruct((LAYERS, NX, NY), F32),
            jax.ShapeDtypeStruct((LAYERS, 2, 8, RUN), F32),
            jax.ShapeDtypeStruct((LAYERS, 2, 8, RUN), F32),
            jax.ShapeDtypeStruct((LAYERS, 8, NY), F32),
            jax.ShapeDtypeStruct((LAYERS, 8, NY), F32),
        ),
        in_specs=[smem] + [vmem] * 5,
        out_specs=(hbm,) * 3 + (vmem,) * 2,
        scratch_shapes=[
            pltpu.VMEM((LAYERS, 2, 8, RUN), F32),
            pltpu.VMEM((LAYERS, 2, 8, RUN), F32),
            pltpu.VMEM((LAYERS, NX, NY), F32),
            pltpu.VMEM((128, RUN), jnp.int32),
            pltpu.SMEM((128, RUN), jnp.int32),
            pltpu.SemaphoreType.DMA,
            pltpu.SemaphoreType.DMA((LAYERS,)),
            pltpu.SemaphoreType.DMA((2,)),
        ]
        + [pltpu.VMEM((POSITIONS + 8, RUN), F32)] * ACCS,
        compiler_params=pltpu.CompilerParams(vmem_limit_bytes=24 * 1024 * 1024),
    )(flags, incoming, left, right, low, high)


def corner_kernel(
    flag_ref, first_in, second_in, low_in, high_in, first_hbm, second_hbm, first_ref, second_ref, sem
):
    even_y = flag_ref[4] > 0
    even_x = flag_ref[5] > 0

    def send(l, h, low, high):
        first_ref[l, h] = jnp.where(even_x, high, low)
        second_ref[l, h] = jnp.where(even_x, low, high)

    lane = iota((8, RUN), 1)
    low = jnp.zeros((8, RUN), F32)
    high = jnp.zeros((8, RUN), F32)
    for l in range(LAYERS):
        for h in range(2):
            cols = slice(h * RUN, (h + 1) * RUN)
            send(l, h, low_in[l, :, cols], high_in[l, :, cols])
        for start, width in FIELDS:
            for side in range(2):
                place = 16 * l + 2 * start + side * width
                chosen = (lane >= place) & (lane < place + width)
                for half in range(2):
                    a = first_in[l, half]
                    b = second_in[l, half]
                    v = jnp.where(even_y, a, b) if side else jnp.where(even_y, b, a)
                    if half == 0:
                        low = jnp.where(chosen, pltpu.roll(v, (place - start) % RUN, 1), low)
                    else:
                        high = jnp.where(chosen, pltpu.roll(v, (place - start - 120) % RUN, 1), high)
    send(LAYERS, 0, low, high)
    sides = [
        pltpu.make_async_copy(first_ref, first_hbm, sem.at[0]),
        pltpu.make_async_copy(second_ref, second_hbm, sem.at[1]),
    ]
    for c in sides:
        c.start()
    for c in sides:
        c.wait()


def corners(flags, first, second, low, high):
    smem = pl.BlockSpec(memory_space=pltpu.SMEM)
    vmem = pl.BlockSpec(memory_space=pltpu.VMEM)
    shape = jax.ShapeDtypeStruct((LAYERS + 1, 2, 8, RUN), F32)
    return pl.pallas_call(
        corner_kernel,
        out_shape=(shape, shape),
        in_specs=[smem] + [vmem] * 4,
        out_specs=(pl.BlockSpec(memory_space=pltpu.HBM),) * 2,
        scratch_shapes=[pltpu.VMEM(shape.shape, F32)] * 2 + [pltpu.SemaphoreType.DMA((2,))],
        compiler_params=pltpu.CompilerParams(vmem_limit_bytes=4 * 1024 * 1024),
    )(flags, first, second, low, high)


def sweep_kernel(
    kind_ref, slope_ref, flag_ref, warmth_hbm, q_hbm, field_hbm, first_y, second_y, first_x, second_x,
    out_hbm,
    warm_a, warm_b, q_ext, field_ext, q_up, q_down, r_next, f_below, g_below, inv_row, sem,
):
    bodies = (warmth_hbm, q_hbm, field_hbm)
    exts = (warm_a, q_ext, field_ext)
    def arriving(k, l):
        return [
            pltpu.make_async_copy(
                bodies[k].at[l, :, pl.ds(h * RUN, RUN)],
                exts[k].at[l, h, pl.ds(BASE, NX), :],
                sem.at[k, l, h],
            )
            for h in range(2)
        ]

    def leaving(l):
        return [
            pltpu.make_async_copy(
                warm_b.at[l, h, pl.ds(BASE, NX), :],
                out_hbm.at[l, :, pl.ds(h * RUN, RUN)],
                sem.at[0, l, h],
            )
            for h in range(2)
        ]

    for l in range(LAYERS):
        for k in range(3):
            for c in arriving(k, l):
                c.start()
    has_left = flag_ref[0] > 0
    has_right = flag_ref[1] > 0
    has_low = flag_ref[2] > 0
    has_high = flag_ref[3] > 0
    even_y = flag_ref[4] > 0
    even_x = flag_ref[5] > 0
    fills = (0.0, WALL, 0.0)
    lane = iota((8, RUN), 1)
    sub = iota((8, RUN), 0)
    first_half = lane < 64

    def halo(l):
        def received(high, h, l):
            a = first_x[l, h]
            b = second_x[l, h]
            return jnp.where(even_x, a, b) if high else jnp.where(even_x, b, a)

        for k, (start, width) in enumerate(FIELDS):
            pick = (lane + 8 - start) % 8 < 4
            for half in range(2):
                a = first_y[l, half]
                b = second_y[l, half]
                v = jnp.where(has_left, jnp.where(even_y, b, a), fills[k])
                w = jnp.where(has_right, jnp.where(even_y, a, b), fills[k])
                both = jnp.where(pick, w, pltpu.roll(v, RUN - width, 1))
                for g in range(16):
                    row = BASE + 8 * (16 * half + g)
                    shift = (RUN - 8 * g - start) % RUN
                    exts[k][l, 2, row : row + 8, :] = pltpu.roll(both, shift, 1)
            for high, present, row in (
                (False, has_low, BASE - width),
                (True, has_high, BASE + NX),
            ):
                for h in range(2):
                    main = jnp.where(present, received(high, h, l), fills[k])
                    exts[k][l, h, row : row + width, :] = main[start : start + width]
                c = received(high, 0, LAYERS)
                c = pltpu.roll(c, RUN - (16 * l + 2 * start + width), 1)
                cl = jnp.where(present & has_left, c, fills[k])
                cr = jnp.where(present & has_right, c, fills[k])
                c = jnp.where(first_half, cr, cl)
                top = 0 if high else 8 - width
                exts[k][l, 2, row : row + width, :] = c[top : top + width]

    last = lane == RUN - 1
    first = lane == 0

    def up(v):
        s = [pltpu.roll(x, RUN - 1, 1) for x in v]
        return [jnp.where(last, s[(h + 1) % 3], s[h]) for h in range(3)]

    def down(v):
        s = [pltpu.roll(x, 1, 1) for x in v]
        return [jnp.where(first, s[(h + 2) % 3], s[h]) for h in range(3)]

    def rcp(x):
        return pl.reciprocal(x, approx=True)

    inverse = [1.0 / jnp.full((8, RUN), slope_ref[kind_ref[l]], F32) for l in range(LAYERS)]
    for l in range(LAYERS):
        inv_row[l] = inverse[l]
    top = BASE - 4
    stride = 33

    def at(j):
        return pl.ds(top + j, 8, stride=stride)

    def load(ref, l, j):
        return [ref[l, h, at(j), :] for h in range(3)]

    def one_sweep(src, dst, opening, blocks):
        every = range(blocks)

        def resist(l, j, t):
            inv = inv_row[l]
            q = load(q_ext, l, j)
            return [q[h] * (t[h] + inv) for h in every]

        def arrive(l):
            for k in range(3):
                for c in arriving(k, l):
                    c.wait()
            halo(l)

        if opening:
            arrive(0)
        for l in range(LAYERS):
            above = l < LAYERS - 1
            if opening and above:
                arrive(l + 1)
            inv = inv_row[l]

            def own(j, t):
                return [r_next[j, h] for h in every] if l > 0 else resist(l, j, t)

            def beside(j, t):
                tu, td = up(t), down(t)
                if opening:
                    q = load(q_ext, l, j)
                    qu, qd = up(q), down(q)
                    for h in range(3):
                        q_up[l, h, at(j), :] = qu[h]
                        q_down[l, h, at(j), :] = qd[h]
                else:
                    qu, qd = load(q_up, l, j), load(q_down, l, j)
                ru = [qu[h] * (tu[h] + inv) for h in every]
                rd = [qd[h] * (td[h] + inv) for h in every]
                return tu, td, ru, rd

            before = load(src, l, -1)
            t = load(src, l, 0)
            r = own(0, t)
            rb = resist(l, -1, before)
            gx = [rcp(rb[h] + r[h]) for h in every]
            px = [gx[h] * before[h] for h in every]
            for j in range(stride):
                tu, td, ru, rd = beside(j, t)
                tn = load(src, l, j + 1)
                rn = own(j + 1, tn)
                if above:
                    ta = load(src, l + 1, j)
                    ra = resist(l + 1, j, ta)
                for h in every:
                    gu = rcp(r[h] + ru[h])
                    gd = rcp(r[h] + rd[h])
                    g = rcp(r[h] + rn[h])
                    numer = field_ext[l, h, at(j), :] + px[h]
                    numer = (numer + g * tn[h]) + (gu * tu[h] + gd * td[h])
                    denom = (g + gx[h]) + (gu + gd)
                    gx[h] = g
                    px[h] = g * t[h]
                    if l > 0:
                        numer = numer + f_below[j, h]
                        denom = denom + g_below[j, h]
                    else:
                        denom = denom + SINK
                    if above:
                        gz = 0.5 * rcp(r[h] + ra[h])
                        numer = numer + gz * ta[h]
                        denom = denom + gz
                        r_next[j, h] = ra[h]
                        g_below[j, h] = gz
                        f_below[j, h] = gz * t[h]
                    dst[l, h, at(j), :] = numer * rcp(denom)
                t = tn
                r = rn
            if above:
                ra = resist(l + 1, stride, load(src, l + 1, stride))
                for h in every:
                    r_next[stride, h] = ra[h]
            if dst is warm_b and not opening:
                for c in leaving(l):
                    c.start()

    one_sweep(warm_a, warm_b, True, 3)
    one_sweep(warm_b, warm_a, False, 3)
    one_sweep(warm_a, warm_b, False, 2)
    for l in range(LAYERS):
        for c in leaving(l):
            c.wait()


def sweeps(kind, slope, flags, warmth, q, field, first_y, second_y, first_x, second_x):
    vmem = pl.BlockSpec(memory_space=pltpu.VMEM)
    smem = pl.BlockSpec(memory_space=pltpu.SMEM)
    hbm = pl.BlockSpec(memory_space=pltpu.HBM)
    ext = pltpu.VMEM((LAYERS, 3, ROWS, RUN), F32)
    row = pltpu.VMEM((34, 3, 8, RUN), F32)
    return pl.pallas_call(
        sweep_kernel,
        out_shape=jax.ShapeDtypeStruct((LAYERS, NX, NY), F32),
        in_specs=[smem, smem, smem, hbm, hbm, hbm, vmem, vmem, vmem, vmem],
        out_specs=hbm,
        scratch_shapes=[
            ext,
            ext,
            ext,
            ext,
            ext,
            ext,
            row,
            row,
            row,
            pltpu.VMEM((LAYERS, 8, RUN), F32),
            pltpu.SemaphoreType.DMA((3, LAYERS, 2)),
        ],
        compiler_params=pltpu.CompilerParams(vmem_limit_bytes=53 * 1024 * 1024),
    )(kind, slope, flags, warmth, q, field, first_y, second_y, first_x, second_x)


def swap(axis, first, second):
    n = lax.axis_size(axis)
    pairs = [(i, i ^ 1) for i in range(n)]
    others = [(i, (((i + 1) ^ 1) - 1) % n) for i in range(n)]
    return lax.ppermute(first, axis, pairs), lax.ppermute(second, axis, others)


def per_device(
    segment_wattage_table,
    segment_target_tile,
    occupied_slot_tally,
    segment_tile_position,
    stratum_substance,
    substance_transport_base,
    substance_thermal_slope,
    thermal_scaling_factor,
    starting_warmth_excess,
):
    tiles = 128
    outgoing = pack(
        occupied_slot_tally,
        segment_target_tile.reshape(-1, RUN),
        segment_tile_position.reshape(-1, RUN),
        segment_wattage_table,
    )
    incoming = lax.all_to_all(
        outgoing.reshape(tiles, 1, CHUNK * RUN), ("gx", "gy"), split_axis=0, concat_axis=0, tiled=True
    ).reshape(tiles * CHUNK, RUN)
    q, left, right, low, high = prepare(
        stratum_substance,
        substance_transport_base,
        substance_thermal_slope,
        starting_warmth_excess,
        thermal_scaling_factor,
    )
    i = lax.axis_index("gx")
    k = lax.axis_index("gy")
    flags = jnp.stack(
        [
            k > 0,
            k < lax.axis_size("gy") - 1,
            i > 0,
            i < lax.axis_size("gx") - 1,
            k % 2 == 0,
            i % 2 == 0,
        ]
    ).astype(jnp.int32)
    field, first, second, low, high = gather(flags, incoming, left, right, low, high)
    first_y, second_y = swap("gy", first, second)
    first, second = corners(flags, first_y, second_y, low, high)
    first_x, second_x = swap("gx", first, second)
    final = sweeps(
        stratum_substance,
        substance_thermal_slope,
        flags,
        starting_warmth_excess,
        q,
        field,
        first_y,
        second_y,
        first_x,
        second_x,
    )
    return field, final


def solution(mesh):
    return jax.shard_map(
        per_device,
        mesh=mesh,
        in_specs=(
            P(("gx", "gy"), None),
            P(("gx", "gy")),
            P(("gx", "gy")),
            P(("gx", "gy")),
            P(),
            P(),
            P(),
            P(None, "gx", "gy"),
            P(None, "gx", "gy"),
        ),
        out_specs=(P(None, "gx", "gy"), P(None, "gx", "gy")),
        check_vma=False,
    )
```

```python
import jax
import jax.numpy as jnp
from jax import lax
from jax.experimental import pallas as pl
from jax.experimental.pallas import tpu as pltpu
from jax.sharding import PartitionSpec as P

RUN = 128
SWEEPS = 3
CAP = 48
CHUNK = CAP + 1
LAYERS = 8
NX = 256
NY = 256
GROUPS = NX // 8
POSITIONS = LAYERS * NX * NY // RUN
ACCS = 6
FIELDS = ((0, 3), (3, 3), (6, 2))
WALL = 1e30
SINK = 4.0
BASE = 16
ROWS = 280
VMEM_LIMIT = 60 * 1024 * 1024
F32 = jnp.float32
BF16 = jnp.bfloat16


def iota(shape, dim):
    return lax.broadcasted_iota(jnp.int32, shape, dim)


def pack_kernel(
    tally_ref, target_ref, place_ref, table_hbm, out_ref, table_ref, dest_v, dest_s, dest_sem, table_sem
):
    load = pltpu.make_async_copy(table_hbm, table_ref, table_sem)
    load.start()
    tally = tally_ref[0]
    tiles = 128
    sub = iota((tiles, RUN), 0)
    lane = iota((1, RUN), 1)
    tri_row = iota((RUN, 2 * RUN), 0)
    tri_col = iota((RUN, 2 * RUN), 1)
    tri = jnp.where((tri_row <= tri_col) | (tri_col >= RUN), 1.0, 0.0).astype(BF16)

    def rank_group(g, carry):
        seen, placed = carry
        live = (lane + g * RUN) < tally
        tgt = target_ref[pl.ds(g, 1), :]
        match = sub == jnp.where(live, tgt, -1)
        onehot = jnp.where(match, 1.0, 0.0)
        run = jnp.dot(onehot.astype(BF16), tri, preferred_element_type=F32)
        rank = jnp.sum(jnp.where(match, seen + run[:, :RUN], 0.0), axis=0, keepdims=True)
        rank = rank.astype(jnp.int32) - 1
        dest_v[pl.ds(g, 1), :] = jnp.where(live, tgt * CHUNK + rank, CAP)
        spot = place_ref[pl.ds(g, 1), :]
        spot = (spot & ~15) | ((spot & 1) << 3) | ((spot >> 1) & 7)
        spot = spot + 1
        digits = jnp.where(sub < 64, spot & 63, spot >> 6)
        chosen = jnp.where((sub & 63) == rank, digits, 0).astype(F32)
        placed = placed + lax.dot_general(
            onehot.astype(BF16),
            chosen.astype(BF16),
            (((1,), (1,)), ((), ())),
            preferred_element_type=F32,
        )
        return seen + run[:, RUN:], placed

    zero = jnp.zeros((tiles, RUN), F32)
    carry = (zero, zero)
    halves = [
        pltpu.make_async_copy(
            dest_v.at[pl.ds(16 * i, 16), :], dest_s.at[pl.ds(16 * i, 16), :], dest_sem.at[i]
        )
        for i in range(2)
    ]
    for i in range(2):
        carry = lax.fori_loop(16 * i, 16 * i + 16, rank_group, carry, unroll=16)
        halves[i].start()
    placed = carry[1] + 64.0 * pltpu.roll(carry[1], 64, 1)

    load.wait()

    def move(g, _):
        for k in range(RUN):
            out_ref[pl.ds(dest_s[g, k], 1), :] = table_ref[pl.ds(g * RUN + k, 1), :]
        return 0

    groups = (tally + RUN - 1) // RUN
    halves[0].wait()
    lax.fori_loop(0, jnp.minimum(groups, 16), move, 0)
    halves[1].wait()
    lax.fori_loop(16, jnp.maximum(groups, 16), move, 0)
    out_ref[pl.ds(CAP, tiles, stride=CHUNK), :] = placed


def pack(tally, target, place, table):
    tiles = 128
    return pl.pallas_call(
        pack_kernel,
        out_shape=jax.ShapeDtypeStruct((tiles * CHUNK, RUN), F32),
        in_specs=[
            pl.BlockSpec(memory_space=pltpu.SMEM),
            pl.BlockSpec(memory_space=pltpu.VMEM),
            pl.BlockSpec(memory_space=pltpu.VMEM),
            pl.BlockSpec(memory_space=pl.ANY),
        ],
        out_specs=pl.BlockSpec(memory_space=pltpu.VMEM),
        scratch_shapes=[
            pltpu.VMEM((32 * RUN, RUN), F32),
            pltpu.VMEM((32, RUN), jnp.int32),
            pltpu.SMEM((32, RUN), jnp.int32),
            pltpu.SemaphoreType.DMA((2,)),
            pltpu.SemaphoreType.DMA,
        ],
        compiler_params=pltpu.CompilerParams(vmem_limit_bytes=VMEM_LIMIT),
    )(tally, target, place, table)


def fold(kept, value, shift, slot, g):
    return jnp.where(slot == g, pltpu.roll(value, shift % RUN, 1), kept)


def prepare_kernel(
    kind_ref, base_ref, slope_ref, warmth_ref, scale_ref, q_ref, left_ref, right_ref, low_ref, high_ref
):
    lane = iota((8, RUN), 1)
    slot = lane // 8
    use_q = lane % 8 >= 3
    sub = iota((8, RUN), 0)

    def layer(l, _):
        kind = kind_ref[l]
        ratio = jnp.full((8, RUN), 0.5 * slope_ref[kind], F32) / jnp.full((8, RUN), base_ref[kind], F32)
        zero = jnp.zeros((8, RUN), F32)
        left = [[zero, zero], [zero, zero]]
        right = [[zero, zero], [zero, zero]]
        for g in range(GROUPS):
            half = g // 16
            k = g % 16
            for h in range(2):
                cols = slice(h * RUN, (h + 1) * RUN)
                t = warmth_ref[l, 8 * g : 8 * g + 8, cols]
                q = ratio / scale_ref[l, 8 * g : 8 * g + 8, cols]
                q_ref[l, 8 * g : 8 * g + 8, cols] = q
                if h == 0:
                    left[half][0] = fold(left[half][0], t, 8 * k, slot, k)
                    left[half][1] = fold(left[half][1], q, 8 * k + 3, slot, k)
                else:
                    right[half][0] = fold(right[half][0], t, 8 * k + 3, slot, k)
                    right[half][1] = fold(right[half][1], q, 8 * k + 6, slot, k)
                if g == 0:
                    low_ref[l, :, cols] = jnp.where(sub < 3, t, pltpu.roll(q, 3, 0))
                if g == GROUPS - 1:
                    high_ref[l, :, cols] = jnp.where(sub < 3, pltpu.roll(t, 3, 0), pltpu.roll(q, 6, 0))
        for half in range(2):
            left_ref[l, half] = jnp.where(use_q, left[half][1], left[half][0])
            right_ref[l, half] = jnp.where(use_q, right[half][1], right[half][0])
        return 0

    lax.fori_loop(0, LAYERS, layer, 0)


def prepare(kind, base, slope, warmth, scale):
    vmem = pl.BlockSpec(memory_space=pltpu.VMEM)
    smem = pl.BlockSpec(memory_space=pltpu.SMEM)
    side = jax.ShapeDtypeStruct((LAYERS, 2, 8, RUN), F32)
    edge = jax.ShapeDtypeStruct((LAYERS, 8, NY), F32)
    return pl.pallas_call(
        prepare_kernel,
        out_shape=(jax.ShapeDtypeStruct(warmth.shape, F32), side, side, edge, edge),
        in_specs=[smem, smem, smem, vmem, vmem],
        out_specs=(vmem,) * 5,
        compiler_params=pltpu.CompilerParams(vmem_limit_bytes=16 * 1024 * 1024),
        cost_estimate=pl.CostEstimate(flops=8000000, bytes_accessed=6300000, transcendentals=0),
    )(kind, base, slope, warmth, scale)


def gather_kernel(
    flag_ref, inc_ref, left_in, right_in, low_in, high_in,
    field_hbm, first_ref, second_ref, low_ref, high_ref,
    field_ref, spot_v, spot_s, spot_sem, field_sem, *accs,
):
    tiles = 128
    marks = inc_ref[pl.ds(CAP, tiles, stride=CHUNK), :]
    spot_v[...] = jnp.where(marks > 0.5, marks.astype(jnp.int32) - 1, POSITIONS)
    copy = pltpu.make_async_copy(spot_v, spot_s, spot_sem)
    copy.start()

    def clear(i, _):
        for acc in accs:
            acc[pl.ds(pl.multiple_of(i * 64, 64), 64), :] = jnp.zeros((64, RUN), F32)
        return 0

    lax.fori_loop(0, POSITIONS // 64, clear, 0)
    copy.wait()

    def source(s, _):
        for p in range(CAP):
            acc = accs[p % ACCS]
            acc[pl.ds(spot_s[s, p], 1), :] += inc_ref[pl.ds(s * CHUNK + p, 1), :]
        return 0

    lax.fori_loop(0, tiles, source, 0, unroll=4)
    even = flag_ref[4] > 0
    lane = iota((8, RUN), 1)
    slot = lane // 8
    use_p = lane % 8 >= 6
    sub = iota((8, RUN), 0)

    def stored(l):
        return pltpu.make_async_copy(field_ref.at[l], field_hbm.at[l], field_sem.at[l])

    def layer(l, _):
        zero = jnp.zeros((8, RUN), F32)
        left = [zero, zero]
        right = [zero, zero]
        for g in range(GROUPS):
            half = g // 16
            k = g % 16
            for h in range(2):
                cols = slice(h * RUN, (h + 1) * RUN)
                start = pl.multiple_of(l * 512 + g * 16 + h * 8, 8)
                v = [acc[pl.ds(start, 8), :] for acc in accs]
                total = ((v[0] + v[1]) + (v[2] + v[3])) + (v[4] + v[5])
                field_ref[l, 8 * g : 8 * g + 8, cols] = total
                if h == 0:
                    left[half] = fold(left[half], total, 8 * k + 6, slot, k)
                else:
                    right[half] = fold(right[half], total, 8 * k + 8, slot, k)
                if g == 0:
                    low_ref[l, :, cols] = jnp.where(sub < 6, low_in[l, :, cols], pltpu.roll(total, 6, 0))
                if g == GROUPS - 1:
                    high_ref[l, :, cols] = jnp.where(sub < 6, high_in[l, :, cols], total)
        for half in range(2):
            lhs = jnp.where(use_p, left[half], left_in[l, half])
            rhs = jnp.where(use_p, right[half], right_in[l, half])
            first_ref[l, half] = jnp.where(even, rhs, lhs)
            second_ref[l, half] = jnp.where(even, lhs, rhs)
        stored(l).start()
        return 0

    lax.fori_loop(0, LAYERS, layer, 0)
    for l in range(LAYERS):
        stored(l).wait()


def gather(flags, incoming, left, right, low, high):
    vmem = pl.BlockSpec(memory_space=pltpu.VMEM)
    hbm = pl.BlockSpec(memory_space=pltpu.HBM)
    smem = pl.BlockSpec(memory_space=pltpu.SMEM)
    return pl.pallas_call(
        gather_kernel,
        out_shape=(
            jax.ShapeDtypeStruct((LAYERS, NX, NY), F32),
            jax.ShapeDtypeStruct((LAYERS, 2, 8, RUN), F32),
            jax.ShapeDtypeStruct((LAYERS, 2, 8, RUN), F32),
            jax.ShapeDtypeStruct((LAYERS, 8, NY), F32),
            jax.ShapeDtypeStruct((LAYERS, 8, NY), F32),
        ),
        in_specs=[smem] + [vmem] * 5,
        out_specs=(hbm,) + (vmem,) * 4,
        scratch_shapes=[
            pltpu.VMEM((LAYERS, NX, NY), F32),
            pltpu.VMEM((128, RUN), jnp.int32),
            pltpu.SMEM((128, RUN), jnp.int32),
            pltpu.SemaphoreType.DMA,
            pltpu.SemaphoreType.DMA((LAYERS,)),
        ]
        + [pltpu.VMEM((POSITIONS + 8, RUN), F32)] * ACCS,
        compiler_params=pltpu.CompilerParams(vmem_limit_bytes=24 * 1024 * 1024),
    )(flags, incoming, left, right, low, high)


def corner_kernel(flag_ref, first_in, second_in, low_in, high_in, first_ref, second_ref):
    even_y = flag_ref[4] > 0
    even_x = flag_ref[5] > 0

    def send(l, h, low, high):
        first_ref[l, h] = jnp.where(even_x, high, low)
        second_ref[l, h] = jnp.where(even_x, low, high)

    lane = iota((8, RUN), 1)
    low = jnp.zeros((8, RUN), F32)
    high = jnp.zeros((8, RUN), F32)
    for l in range(LAYERS):
        for h in range(2):
            cols = slice(h * RUN, (h + 1) * RUN)
            send(l, h, low_in[l, :, cols], high_in[l, :, cols])
        for start, width in FIELDS:
            for side in range(2):
                place = 16 * l + 2 * start + side * width
                chosen = (lane >= place) & (lane < place + width)
                for half in range(2):
                    a = first_in[l, half]
                    b = second_in[l, half]
                    v = jnp.where(even_y, a, b) if side else jnp.where(even_y, b, a)
                    if half == 0:
                        low = jnp.where(chosen, pltpu.roll(v, (place - start) % RUN, 1), low)
                    else:
                        high = jnp.where(chosen, pltpu.roll(v, (place - start - 120) % RUN, 1), high)
    send(LAYERS, 0, low, high)
    blank = jnp.zeros((8, RUN), F32)
    first_ref[LAYERS, 1] = blank
    second_ref[LAYERS, 1] = blank


def corners(flags, first, second, low, high):
    smem = pl.BlockSpec(memory_space=pltpu.SMEM)
    vmem = pl.BlockSpec(memory_space=pltpu.VMEM)
    shape = jax.ShapeDtypeStruct((LAYERS + 1, 2, 8, RUN), F32)
    return pl.pallas_call(
        corner_kernel,
        out_shape=(shape, shape),
        in_specs=[smem] + [vmem] * 4,
        out_specs=(vmem,) * 2,
        compiler_params=pltpu.CompilerParams(vmem_limit_bytes=4 * 1024 * 1024),
    )(flags, first, second, low, high)


def sweep_kernel(
    kind_ref, slope_ref, flag_ref, warmth_hbm, q_hbm, field_hbm, first_y, second_y, first_x, second_x,
    out_hbm,
    warm_a, warm_b, q_ext, field_ext, q_up, q_down, r_next, f_below, g_below, inv_row, sem,
):
    bodies = (warmth_hbm, q_hbm, field_hbm)
    exts = (warm_a, q_ext, field_ext)
    def arriving(k, l):
        return [
            pltpu.make_async_copy(
                bodies[k].at[l, :, pl.ds(h * RUN, RUN)],
                exts[k].at[l, h, pl.ds(BASE, NX), :],
                sem.at[k, l, h],
            )
            for h in range(2)
        ]

    def leaving(l):
        return [
            pltpu.make_async_copy(
                warm_b.at[l, h, pl.ds(BASE, NX), :],
                out_hbm.at[l, :, pl.ds(h * RUN, RUN)],
                sem.at[0, l, h],
            )
            for h in range(2)
        ]

    for l in range(LAYERS):
        for k in range(3):
            for c in arriving(k, l):
                c.start()
    has_left = flag_ref[0] > 0
    has_right = flag_ref[1] > 0
    has_low = flag_ref[2] > 0
    has_high = flag_ref[3] > 0
    even_y = flag_ref[4] > 0
    even_x = flag_ref[5] > 0
    fills = (0.0, WALL, 0.0)
    lane = iota((8, RUN), 1)
    sub = iota((8, RUN), 0)
    first_half = lane < 64

    def halo(l):
        def received(high, h, l):
            a = first_x[l, h]
            b = second_x[l, h]
            return jnp.where(even_x, a, b) if high else jnp.where(even_x, b, a)

        for k, (start, width) in enumerate(FIELDS):
            pick = (lane + 8 - start) % 8 < 4
            for half in range(2):
                a = first_y[l, half]
                b = second_y[l, half]
                v = jnp.where(has_left, jnp.where(even_y, b, a), fills[k])
                w = jnp.where(has_right, jnp.where(even_y, a, b), fills[k])
                both = jnp.where(pick, w, pltpu.roll(v, RUN - width, 1))
                for g in range(16):
                    row = BASE + 8 * (16 * half + g)
                    shift = (RUN - 8 * g - start) % RUN
                    exts[k][l, 2, row : row + 8, :] = pltpu.roll(both, shift, 1)
            for high, present, row in (
                (False, has_low, BASE - width),
                (True, has_high, BASE + NX),
            ):
                for h in range(2):
                    main = jnp.where(present, received(high, h, l), fills[k])
                    exts[k][l, h, row : row + width, :] = main[start : start + width]
                c = received(high, 0, LAYERS)
                c = pltpu.roll(c, RUN - (16 * l + 2 * start + width), 1)
                cl = jnp.where(present & has_left, c, fills[k])
                cr = jnp.where(present & has_right, c, fills[k])
                c = jnp.where(first_half, cr, cl)
                top = 0 if high else 8 - width
                exts[k][l, 2, row : row + width, :] = c[top : top + width]

    last = lane == RUN - 1
    first = lane == 0

    def up(v):
        s = [pltpu.roll(x, RUN - 1, 1) for x in v]
        return [jnp.where(last, s[(h + 1) % 3], s[h]) for h in range(3)]

    def down(v):
        s = [pltpu.roll(x, 1, 1) for x in v]
        return [jnp.where(first, s[(h + 2) % 3], s[h]) for h in range(3)]

    def rcp(x):
        return pl.reciprocal(x, approx=True)

    inverse = [1.0 / jnp.full((8, RUN), slope_ref[kind_ref[l]], F32) for l in range(LAYERS)]
    for l in range(LAYERS):
        inv_row[l] = inverse[l]
    top = BASE - 4
    stride = 33

    def at(j):
        return pl.ds(top + j, 8, stride=stride)

    def load(ref, l, j):
        return [ref[l, h, at(j), :] for h in range(3)]

    def one_sweep(src, dst, opening, blocks):
        every = range(blocks)

        def resist(l, j, t):
            inv = inv_row[l]
            q = load(q_ext, l, j)
            return [q[h] * (t[h] + inv) for h in every]

        def arrive(l):
            for k in range(3):
                for c in arriving(k, l):
                    c.wait()
            halo(l)

        if opening:
            arrive(0)
        for l in range(LAYERS):
            above = l < LAYERS - 1
            if opening and above:
                arrive(l + 1)
            inv = inv_row[l]

            def own(j, t):
                return [r_next[j, h] for h in every] if l > 0 else resist(l, j, t)

            def beside(j, t):
                tu, td = up(t), down(t)
                if opening:
                    q = load(q_ext, l, j)
                    qu, qd = up(q), down(q)
                    for h in range(3):
                        q_up[l, h, at(j), :] = qu[h]
                        q_down[l, h, at(j), :] = qd[h]
                else:
                    qu, qd = load(q_up, l, j), load(q_down, l, j)
                ru = [qu[h] * (tu[h] + inv) for h in every]
                rd = [qd[h] * (td[h] + inv) for h in every]
                return tu, td, ru, rd

            before = load(src, l, -1)
            t = load(src, l, 0)
            r = own(0, t)
            rb = resist(l, -1, before)
            gx = [rcp(rb[h] + r[h]) for h in every]
            px = [gx[h] * before[h] for h in every]
            for j in range(stride):
                tu, td, ru, rd = beside(j, t)
                tn = load(src, l, j + 1)
                rn = own(j + 1, tn)
                if above:
                    ta = load(src, l + 1, j)
                    ra = resist(l + 1, j, ta)
                for h in every:
                    gu = rcp(r[h] + ru[h])
                    gd = rcp(r[h] + rd[h])
                    g = rcp(r[h] + rn[h])
                    numer = field_ext[l, h, at(j), :] + px[h]
                    numer = (numer + g * tn[h]) + (gu * tu[h] + gd * td[h])
                    denom = (g + gx[h]) + (gu + gd)
                    gx[h] = g
                    px[h] = g * t[h]
                    if l > 0:
                        numer = numer + f_below[j, h]
                        denom = denom + g_below[j, h]
                    else:
                        denom = denom + SINK
                    if above:
                        gz = 0.5 * rcp(r[h] + ra[h])
                        numer = numer + gz * ta[h]
                        denom = denom + gz
                        r_next[j, h] = ra[h]
                        g_below[j, h] = gz
                        f_below[j, h] = gz * t[h]
                    dst[l, h, at(j), :] = numer * rcp(denom)
                t = tn
                r = rn
            if above:
                ra = resist(l + 1, stride, load(src, l + 1, stride))
                for h in every:
                    r_next[stride, h] = ra[h]
            if dst is warm_b and not opening:
                for c in leaving(l):
                    c.start()

    one_sweep(warm_a, warm_b, True, 3)
    one_sweep(warm_b, warm_a, False, 3)
    one_sweep(warm_a, warm_b, False, 2)
    for l in range(LAYERS):
        for c in leaving(l):
            c.wait()


def sweeps(kind, slope, flags, warmth, q, field, first_y, second_y, first_x, second_x):
    vmem = pl.BlockSpec(memory_space=pltpu.VMEM)
    smem = pl.BlockSpec(memory_space=pltpu.SMEM)
    hbm = pl.BlockSpec(memory_space=pltpu.HBM)
    ext = pltpu.VMEM((LAYERS, 3, ROWS, RUN), F32)
    row = pltpu.VMEM((34, 3, 8, RUN), F32)
    return pl.pallas_call(
        sweep_kernel,
        out_shape=jax.ShapeDtypeStruct((LAYERS, NX, NY), F32),
        in_specs=[smem, smem, smem, hbm, hbm, hbm, vmem, vmem, vmem, vmem],
        out_specs=hbm,
        scratch_shapes=[
            ext,
            ext,
            ext,
            ext,
            ext,
            ext,
            row,
            row,
            row,
            pltpu.VMEM((LAYERS, 8, RUN), F32),
            pltpu.SemaphoreType.DMA((3, LAYERS, 2)),
        ],
        compiler_params=pltpu.CompilerParams(vmem_limit_bytes=53 * 1024 * 1024),
    )(kind, slope, flags, warmth, q, field, first_y, second_y, first_x, second_x)


def swap(axis, first, second):
    n = lax.axis_size(axis)
    pairs = [(i, i ^ 1) for i in range(n)]
    others = [(i, (((i + 1) ^ 1) - 1) % n) for i in range(n)]
    return lax.ppermute(first, axis, pairs), lax.ppermute(second, axis, others)


def per_device(
    segment_wattage_table,
    segment_target_tile,
    occupied_slot_tally,
    segment_tile_position,
    stratum_substance,
    substance_transport_base,
    substance_thermal_slope,
    thermal_scaling_factor,
    starting_warmth_excess,
):
    tiles = 128
    outgoing = pack(
        occupied_slot_tally,
        segment_target_tile.reshape(-1, RUN),
        segment_tile_position.reshape(-1, RUN),
        segment_wattage_table,
    )
    incoming = lax.all_to_all(
        outgoing.reshape(tiles, 1, CHUNK * RUN), ("gx", "gy"), split_axis=0, concat_axis=0, tiled=True
    ).reshape(tiles * CHUNK, RUN)
    q, left, right, low, high = prepare(
        stratum_substance,
        substance_transport_base,
        substance_thermal_slope,
        starting_warmth_excess,
        thermal_scaling_factor,
    )
    i = lax.axis_index("gx")
    k = lax.axis_index("gy")
    flags = jnp.stack(
        [
            k > 0,
            k < lax.axis_size("gy") - 1,
            i > 0,
            i < lax.axis_size("gx") - 1,
            k % 2 == 0,
            i % 2 == 0,
        ]
    ).astype(jnp.int32)
    field, first, second, low, high = gather(flags, incoming, left, right, low, high)
    first_y, second_y = swap("gy", first, second)
    first, second = corners(flags, first_y, second_y, low, high)
    first_x, second_x = swap("gx", first, second)
    final = sweeps(
        stratum_substance,
        substance_thermal_slope,
        flags,
        starting_warmth_excess,
        q,
        field,
        first_y,
        second_y,
        first_x,
        second_x,
    )
    return field, final


def solution(mesh):
    return jax.shard_map(
        per_device,
        mesh=mesh,
        in_specs=(
            P(("gx", "gy"), None),
            P(("gx", "gy")),
            P(("gx", "gy")),
            P(("gx", "gy")),
            P(),
            P(),
            P(),
            P(None, "gx", "gy"),
            P(None, "gx", "gy"),
        ),
        out_specs=(P(None, "gx", "gy"), P(None, "gx", "gy")),
        check_vma=False,
    )
```
